32 devices in a mesh: fsdp: 32 (over z, y, x, core).
Axes of the slice: x: 2, y: 2, z: 4, core: 2. Of those that a mesh axis runs over, the one named last changes fastest.
Arguments:
- tokens: bfloat16 [8192, 576], P('fsdp'), may hold values from -6 to 6
- segments: int32 [8192], P('fsdp'), may hold values from -1 to 8191, as said below
- w_query: bfloat16 [331776], P('fsdp'), may hold values from -0.25 to 0.25
- w_key: bfloat16 [110592], P('fsdp'), may hold values from -0.25 to 0.25
- w_value: bfloat16 [110592], P('fsdp'), may hold values from -0.25 to 0.25
- w_output: bfloat16 [331776], P('fsdp'), may hold values from -0.75 to 0.75
- w_gate: bfloat16 [884736], P('fsdp'), may hold values from -0.25 to 0.25
- w_up: bfloat16 [884736], P('fsdp'), may hold values from -0.25 to 0.25
- w_down: bfloat16 [884736], P('fsdp'), may hold values from -0.15625 to 0.15625
- gains: bfloat16 [1152], P('fsdp'), may hold values from 0.099609375 to 1.8984375
- cotangent: bfloat16 [8192, 576], P('fsdp'), may hold values from -6 to 6
Outputs:
- output_tokens: bfloat16 [8192, 576], P('fsdp')
- grad_tokens: bfloat16 [8192, 576], P('fsdp')
- grad_query: float32 [331776], P('fsdp')
- grad_key: float32 [110592], P('fsdp')
- grad_value: float32 [110592], P('fsdp')
- grad_output: float32 [331776], P('fsdp')
- grad_gate: float32 [884736], P('fsdp')
- grad_up: float32 [884736], P('fsdp')
- grad_down: float32 [884736], P('fsdp')
- grad_gains: float32 [1152], P('fsdp')
The draws below stay inside these ranges and needn't reach their ends.
Inputs may be any that keep to these rules, and one draw needn't show every extreme that they name: `segments`: each block of 256 slots holds whole sequences one after another, then -1 in unused slots at its end; a sequence's number is the index in the whole array of its last slot. Every block has at least 64 used slots, the last block is full, and in every draw one block holds a single sequence of 256 tokens.
All inputs are finite; a program needn't handle non-finite values.
Results may differ from the reference program's by a relative error of at most 0.012.
Values may be sent and summed in bfloat16 or wider, within the bound.
A program may use at most 128 MiB of HBM per device.

```python
import jax
import jax.numpy as jnp
from jax import lax

HEADS = 9
KV_HEADS = 3
HEAD_DIM = 64
FF = 1536
TOK_DEV = 256
D = 576
KV = 192
TOKENS = 8192
GAIN_LEN = 1152


def draw_segments(key, part):
    key = jax.random.fold_in(key, 7)
    device_count = TOKENS // TOK_DEV
    load_key, pick_key, split_key = jax.random.split(key, 3)
    device_loads = jax.random.randint(load_key, (device_count,), TOK_DEV // 4, TOK_DEV + 1)
    chosen = jax.random.randint(pick_key, (), 0, device_count)
    device_ids = jnp.arange(device_count)
    device_loads = jnp.where((device_ids == chosen) | (device_ids == device_count - 1), TOK_DEV, device_loads)
    slot_ids = jnp.arange(TOK_DEV)
    breaks = jax.random.randint(split_key, (device_count, TOK_DEV), 0, max(TOK_DEV // 4, 2)) == 0
    breaks = breaks & (device_ids != chosen)[:, None]
    starts = (slot_ids == 0)[None, :] | breaks
    filled = slot_ids[None, :] < device_loads[:, None]
    next_starts = jnp.concatenate([starts[:, 1:], jnp.ones((device_count, 1), bool)], axis=1)
    next_filled = jnp.concatenate([filled[:, 1:], jnp.zeros((device_count, 1), bool)], axis=1)
    ends = filled & (next_starts | jnp.logical_not(next_filled))
    flat_index = jnp.arange(TOKENS).astype(jnp.int32)
    end_marks = jnp.where(ends.reshape(-1), flat_index, TOKENS).astype(jnp.int32)
    numbers = lax.cummin(end_marks, axis=0, reverse=True)
    return jnp.where(filled.reshape(-1), numbers, -1).astype(jnp.int32)


def level_of(own_key, dims, cuts, low, top_value):
    loudness, own = 1.0, jax.random.fold_in(own_key, 6)
    for dim, blocks in cuts:
        heights = jnp.exp(jax.random.uniform(jax.random.fold_in(own, dim), (blocks,), jnp.float32, low / len(cuts), top_value / len(cuts)))
        loudness = loudness * jnp.repeat(heights, dims[dim] // blocks).reshape([-1 if axis == dim else 1 for axis in range(len(dims))])
    return loudness


def bell_draw(stream_key, extent, spread, bound, cuts=(), dtype=jnp.bfloat16):
    gain = level_of(stream_key, extent, cuts, -0.22, 0.18) if cuts else 1.0
    drawn = jax.random.normal(stream_key, extent, jnp.float32) * spread * gain
    return jnp.minimum(jnp.maximum(drawn, -bound), bound).astype(dtype)


def setup_inputs(seed: int = 0) -> dict:
    seeds = jax.random.split(jax.random.key(seed), 12)
    return {
        "tokens": bell_draw(seeds[0], (TOKENS, D), 1.0, 6.0, ((0, 32),)),
        "segments": draw_segments(jax.random.fold_in(seeds[11], 71), 0),
        "w_query": bell_draw(seeds[2], (D * D,), D ** -0.5, 0.25, ((0, 32),)),
        "w_key": bell_draw(seeds[3], (D * KV,), D ** -0.5, 0.25, ((0, 32),)),
        "w_value": bell_draw(seeds[4], (D * KV,), D ** -0.5, 0.25, ((0, 32),)),
        "w_output": bell_draw(seeds[5], (D * D,), (D // 8) ** -0.5, 0.75, ((0, 32),)),
        "w_gate": bell_draw(seeds[6], (D * FF,), D ** -0.5, 0.25, ((0, 32),)),
        "w_up": bell_draw(seeds[7], (D * FF,), D ** -0.5, 0.25, ((0, 32),)),
        "w_down": bell_draw(seeds[8], (FF * D,), FF ** -0.5, 0.15625, ((0, 32),)),
        "gains": jnp.clip(1.0 + 0.18 * jax.random.normal(seeds[9], (GAIN_LEN,), jnp.float32), 0.099609375, 1.8984375).astype(jnp.bfloat16),
        "cotangent": bell_draw(seeds[10], (TOKENS, D), 1.0, 6.0, ((0, 32),)),
    }


ROPE_BASE = 100000.0
NORM_EPSILON = 1e-05
NEG_LARGE = -1e+30
HIGHEST = lax.Precision.HIGHEST

@jax.custom_vjp
def low(v):
    return lax.optimization_barrier(v.astype(jnp.bfloat16)).astype(jnp.float32)

@jax.custom_vjp
def low_back(v):
    return v

def low_keep(v):
    return (low(v), None)

def low_pass(kept, grad):
    return (grad,)

def back_keep(v):
    return (v, None)

def back_low(kept, grad):
    return (low(grad),)
low.defvjp(low_keep, low_pass)
low_back.defvjp(back_keep, back_low)

def matmul(left, right):
    return jnp.dot(left, right, precision=HIGHEST)

def normalize(values):
    return values * lax.rsqrt(lax.optimization_barrier(jnp.mean(values * values, axis=-1, keepdims=True)) + NORM_EPSILON)

def rotate(values, cosine, sine_table):
    half_dim = values.shape[-1] // 2
    first_half = values[..., :half_dim]
    second_half = values[..., half_dim:]
    return jnp.concatenate([first_half * cosine - second_half * sine_table, second_half * cosine + first_half * sine_table], axis=-1)

def tables(segment_ids):
    token_count = segment_ids.shape[0]
    column = jnp.arange(token_count)[None, :]
    row_index = jnp.arange(token_count)[:, None]
    same_segment = segment_ids[:, None] == segment_ids[None, :]
    positions = lax.optimization_barrier(jnp.sum((same_segment & (column < row_index)).astype(jnp.int32), axis=1))
    allowed = same_segment & (column <= row_index)
    frequency = ROPE_BASE ** (-(2.0 * jnp.arange(HEAD_DIM // 2).astype(jnp.float32)) / HEAD_DIM)
    angles = positions.astype(jnp.float32)[:, None] * frequency[None, :]
    return (allowed, jnp.cos(angles)[:, None, :], jnp.sin(angles)[:, None, :])

def layer_block(weights, tokens, segment_ids):
    w_query, w_key, w_value, w_output, w_gate, w_up, w_down, gains = weights
    group_size = HEADS // KV_HEADS
    token_count = tokens.shape[0]
    allowed, cosine, sine_table = tables(segment_ids)
    normed = low(normalize(tokens) * gains[:D])
    query_pre = low_back(matmul(normed, w_query.reshape(D, D)))
    key_pre = low_back(matmul(normed, w_key.reshape(D, KV)))
    values_low = low(low_back(matmul(normed, w_value.reshape(D, KV)))).reshape(token_count, KV_HEADS, HEAD_DIM)
    queries = low(rotate(query_pre.reshape(token_count, HEADS, HEAD_DIM), cosine, sine_table))
    queries = queries.reshape(token_count, KV_HEADS, group_size, HEAD_DIM)
    keys_rot = low(rotate(key_pre.reshape(token_count, KV_HEADS, HEAD_DIM), cosine, sine_table))
    score_scale = HEAD_DIM ** (-0.5)
    scores = low_back(jnp.einsum('qkgd,tkd->kgqt', queries, keys_rot, precision=HIGHEST) * score_scale)
    scores = jnp.where(allowed, scores, NEG_LARGE)
    row_peak = lax.optimization_barrier(jnp.max(scores, axis=-1, keepdims=True))
    exponentials = jnp.exp(scores - row_peak)
    probabilities = low(exponentials / lax.optimization_barrier(jnp.sum(exponentials, axis=-1, keepdims=True)))
    attended = jnp.einsum('kgqt,tkd->qkgd', probabilities, values_low, precision=HIGHEST).reshape(token_count, D)
    attended = low(low_back(attended))
    branch = low_back(matmul(attended, w_output.reshape(D, D)))
    middle = tokens + branch
    normed_two = low(normalize(middle) * gains[D:2 * D])
    gate_pre = low_back(matmul(normed_two, w_gate.reshape(D, FF)))
    up_pre = low_back(matmul(normed_two, w_up.reshape(D, FF)))
    product = low(jax.nn.silu(gate_pre) * up_pre)
    return middle + low_back(matmul(product, w_down.reshape(FF, D)))

def reference(tokens, segments, w_query, w_key, w_value, w_output, w_gate, w_up, w_down, gains, cotangent):
    device_count = TOKENS // TOK_DEV
    live_rows = (segments >= 0).astype(jnp.float32)[:, None]
    blocked_ids = segments.reshape(device_count, TOK_DEV)

    def forward(token_values, weights):
        block_step = jax.checkpoint(lambda block_pair: layer_block(weights, block_pair[0], block_pair[1]))
        outputs = lax.map(block_step, (token_values.reshape(device_count, TOK_DEV, D), blocked_ids))
        return outputs.reshape(TOKENS, D)
    weights = tuple((item_array.astype(jnp.float32) for item_array in (w_query, w_key, w_value, w_output, w_gate, w_up, w_down, gains)))
    result, pullback = jax.vjp(forward, tokens.astype(jnp.float32), weights)
    grad_in, grad_weights = pullback(cotangent.astype(jnp.float32) * live_rows)
    return ((result * live_rows).astype(jnp.bfloat16), grad_in.astype(jnp.bfloat16), grad_weights[0], grad_weights[1], grad_weights[2], grad_weights[3], grad_weights[4], grad_weights[5], grad_weights[6], grad_weights[7])
```

```python
import jax
import jax.numpy as jnp
import ml_dtypes
import numpy as np
from jax import lax
from jax.experimental import pallas as pl
from jax.experimental.pallas import tpu as pltpu
from jax.sharding import PartitionSpec as P

HEADS = 9
KV_HEADS = 3
HEAD_DIM = 64
FF = 1536
D = 576
KV = 192


ROPE_BASE = 100000.0
NORM_EPSILON = 1e-05
NEG_LARGE = -1e30


def unpack(flat_arrays):
    return (
        flat_arrays[0].reshape(D, D),
        flat_arrays[1].reshape(D, KV),
        flat_arrays[2].reshape(D, KV),
        flat_arrays[3].reshape(D, D),
        flat_arrays[4].reshape(D, FF),
        flat_arrays[5].reshape(D, FF),
        flat_arrays[6].reshape(FF, D),
        flat_arrays[7][:D].astype(jnp.float32),
        flat_arrays[7][D : 2 * D].astype(jnp.float32),
    )


def normalize_parts(values):
    inverse_root = lax.rsqrt(jnp.mean(values * values, axis=-1, keepdims=True) + NORM_EPSILON)
    return (values * inverse_root, inverse_root)


def norm_backward(grad_in, normed, inverse_root, gain_row):
    scaled = grad_in * gain_row
    return inverse_root * (scaled - normed * jnp.mean(scaled * normed, axis=-1, keepdims=True))


def rotate(values, cosine, sine_table):
    half_dim = values.shape[-1] // 2
    first_half = values[..., :half_dim]
    second_half = values[..., half_dim:]
    return jnp.concatenate(
        [
            first_half * cosine - second_half * sine_table,
            second_half * cosine + first_half * sine_table,
        ],
        axis=-1,
    )


def rotate_back(values, cosine, sine_table):
    half_dim = values.shape[-1] // 2
    first_half = values[..., :half_dim]
    second_half = values[..., half_dim:]
    return jnp.concatenate(
        [
            first_half * cosine + second_half * sine_table,
            second_half * cosine - first_half * sine_table,
        ],
        axis=-1,
    )


def per_device(
    tokens, segments, w_query, w_key, w_value, w_output, w_gate, w_up, w_down, gains, cotangent
):
    token_count = tokens.shape[0]
    group_size = HEADS // KV_HEADS
    score_scale = HEAD_DIM ** (-0.5)
    gain_length = gains.shape[0] * lax.axis_size("fsdp")
    gathered = (
        lax.all_gather(w_query, "fsdp", axis=0, tiled=True),
        lax.all_gather(w_key, "fsdp", axis=0, tiled=True),
        lax.all_gather(w_value, "fsdp", axis=0, tiled=True),
        lax.all_gather(w_output, "fsdp", axis=0, tiled=True),
        lax.all_gather(w_gate, "fsdp", axis=0, tiled=True),
        lax.all_gather(w_up, "fsdp", axis=0, tiled=True),
        lax.all_gather(w_down, "fsdp", axis=0, tiled=True),
        lax.all_gather(gains, "fsdp", axis=0, tiled=True),
    )
    (
        query_matrix,
        key_matrix,
        value_matrix,
        output_matrix,
        gate_matrix,
        up_matrix,
        down_matrix,
        gain_first,
        gain_second,
    ) = unpack(gathered)
    column = jnp.arange(token_count)[None, :]
    row_index = jnp.arange(token_count)[:, None]
    same_segment = segments[:, None] == segments[None, :]
    positions = jnp.sum((same_segment & (column < row_index)).astype(jnp.int32), axis=1)
    allowed = same_segment & (column <= row_index)
    frequency = ROPE_BASE ** (-(2.0 * jnp.arange(HEAD_DIM // 2).astype(jnp.float32)) / HEAD_DIM)
    angles = positions.astype(jnp.float32)[:, None] * frequency[None, :]
    cosine = jnp.cos(angles)[:, None, :]
    sine_table = jnp.sin(angles)[:, None, :]
    live_rows = (segments >= 0).astype(jnp.float32)[:, None]
    token_values = tokens.astype(jnp.float32)
    normed_one, root_one = normalize_parts(token_values)
    input_one = (normed_one * gain_first).astype(jnp.bfloat16)
    query_pre = jnp.dot(input_one, query_matrix, preferred_element_type=jnp.float32)
    key_pre = jnp.dot(input_one, key_matrix, preferred_element_type=jnp.float32)
    value_low = jnp.dot(input_one, value_matrix, preferred_element_type=jnp.float32).astype(
        jnp.bfloat16
    )
    value_low = value_low.reshape(token_count, KV_HEADS, HEAD_DIM)
    query_low = rotate(query_pre.reshape(token_count, HEADS, HEAD_DIM), cosine, sine_table).astype(
        jnp.bfloat16
    )
    query_low = query_low.reshape(token_count, KV_HEADS, group_size, HEAD_DIM)
    key_low = rotate(key_pre.reshape(token_count, KV_HEADS, HEAD_DIM), cosine, sine_table).astype(
        jnp.bfloat16
    )
    block_rows = min(token_count, 512)
    block_count = token_count // block_rows

    def masked_scores():
        scores = (
            jnp.einsum("qkgd,tkd->kgqt", query_low, key_low, preferred_element_type=jnp.float32)
            * score_scale
        )
        return (query_low, jnp.where(allowed, scores, NEG_LARGE))

    def attend(block_index):
        query_block, scores = masked_scores()
        row_peak = jnp.max(scores, axis=-1, keepdims=True)
        exponentials = jnp.exp(scores - row_peak)
        totals = jnp.sum(exponentials, axis=-1, keepdims=True)
        probabilities = (exponentials / totals).astype(jnp.bfloat16)
        attended = jnp.einsum(
            "kgqt,tkd->qkgd", probabilities, value_low, preferred_element_type=jnp.float32
        )
        return (attended.astype(jnp.bfloat16), row_peak[..., 0] + jnp.log(totals[..., 0]))

    attended_blocks, log_totals = lax.map(attend, jnp.arange(block_count))
    attended_low = attended_blocks.reshape(token_count, D)
    branch = jnp.dot(attended_low, output_matrix, preferred_element_type=jnp.float32)
    middle = token_values + branch
    normed_two, root_two = normalize_parts(middle)
    input_two = (normed_two * gain_second).astype(jnp.bfloat16)
    gate_pre = jnp.dot(input_two, gate_matrix, preferred_element_type=jnp.float32)
    up_pre = jnp.dot(input_two, up_matrix, preferred_element_type=jnp.float32)
    sigmoid_gate = jax.nn.sigmoid(gate_pre)
    silu_gate = gate_pre * sigmoid_gate
    product_low = (silu_gate * up_pre).astype(jnp.bfloat16)
    result = middle + jnp.dot(product_low, down_matrix, preferred_element_type=jnp.float32)
    output_tokens = (result * live_rows).astype(jnp.bfloat16)
    regathered = (
        lax.all_gather(w_query, "fsdp", axis=0, tiled=True),
        lax.all_gather(w_key, "fsdp", axis=0, tiled=True),
        lax.all_gather(w_value, "fsdp", axis=0, tiled=True),
        lax.all_gather(w_output, "fsdp", axis=0, tiled=True),
        lax.all_gather(w_gate, "fsdp", axis=0, tiled=True),
        lax.all_gather(w_up, "fsdp", axis=0, tiled=True),
        lax.all_gather(w_down, "fsdp", axis=0, tiled=True),
        lax.all_gather(gains, "fsdp", axis=0, tiled=True),
    )
    back_weights = unpack(regathered)
    (
        back_query,
        back_key,
        back_value,
        back_output,
        back_gate,
        back_up,
        back_down,
        back_first,
        back_second,
    ) = back_weights
    grad_result = cotangent.astype(jnp.float32) * live_rows
    grad_down_in = grad_result.astype(jnp.bfloat16)
    grad_down = jnp.einsum(
        "tf,td->fd", product_low, grad_down_in, preferred_element_type=jnp.float32
    )
    grad_product = jnp.einsum(
        "td,fd->tf", grad_down_in, back_down, preferred_element_type=jnp.float32
    )
    grad_gate_pre = (
        grad_product * up_pre * sigmoid_gate * (1.0 + gate_pre * (1.0 - sigmoid_gate))
    ).astype(jnp.bfloat16)
    grad_up_pre = (grad_product * silu_gate).astype(jnp.bfloat16)
    grad_gate = jnp.einsum(
        "td,tf->df", input_two, grad_gate_pre, preferred_element_type=jnp.float32
    )
    grad_up = jnp.einsum("td,tf->df", input_two, grad_up_pre, preferred_element_type=jnp.float32)
    grad_input_two = jnp.einsum(
        "tf,df->td", grad_gate_pre, back_gate, preferred_element_type=jnp.float32
    )
    grad_input_two = grad_input_two + jnp.einsum(
        "tf,df->td", grad_up_pre, back_up, preferred_element_type=jnp.float32
    )
    grad_gain_two = jnp.sum(grad_input_two * normed_two, axis=0)
    grad_middle = grad_result + norm_backward(grad_input_two, normed_two, root_two, back_second)
    grad_branch = grad_middle.astype(jnp.bfloat16)
    grad_output = jnp.einsum(
        "td,te->de", attended_low, grad_branch, preferred_element_type=jnp.float32
    )
    grad_attended = jnp.einsum(
        "te,de->td", grad_branch, back_output, preferred_element_type=jnp.float32
    ).astype(jnp.bfloat16)
    grad_attended = grad_attended.reshape(token_count, KV_HEADS, group_size, HEAD_DIM)

    def back_step(carried, inputs):
        grad_keys, grad_values = carried
        block_index, log_block = inputs
        query_block, scores = masked_scores()
        probabilities = jnp.exp(scores - log_block[..., None])
        grad_probs = jnp.einsum(
            "qkgd,tkd->kgqt", grad_attended, value_low, preferred_element_type=jnp.float32
        )
        centre = jnp.sum(probabilities * grad_probs, axis=-1, keepdims=True)
        grad_scores = (probabilities * (grad_probs - centre)).astype(jnp.bfloat16)
        grad_query_block = (
            jnp.einsum("kgqt,tkd->qkgd", grad_scores, key_low, preferred_element_type=jnp.float32)
            * score_scale
        )
        grad_keys = (
            grad_keys
            + jnp.einsum(
                "kgqt,qkgd->tkd", grad_scores, query_block, preferred_element_type=jnp.float32
            )
            * score_scale
        )
        grad_values = grad_values + jnp.einsum(
            "kgqt,qkgd->tkd",
            probabilities.astype(jnp.bfloat16),
            grad_attended,
            preferred_element_type=jnp.float32,
        )
        return ((grad_keys, grad_values), grad_query_block)

    zero_state = jnp.zeros((token_count, KV_HEADS, HEAD_DIM), jnp.float32)
    (grad_keys, grad_values), grad_query_blocks = lax.scan(
        back_step, (zero_state, zero_state), (jnp.arange(block_count), log_totals)
    )
    grad_query_low = rotate_back(
        grad_query_blocks.reshape(token_count, HEADS, HEAD_DIM), cosine, sine_table
    )
    grad_query_low = grad_query_low.astype(jnp.bfloat16).reshape(token_count, D)
    grad_key_low = (
        rotate_back(grad_keys, cosine, sine_table).astype(jnp.bfloat16).reshape(token_count, KV)
    )
    grad_value_low = grad_values.astype(jnp.bfloat16).reshape(token_count, KV)
    grad_query = jnp.einsum(
        "td,te->de", input_one, grad_query_low, preferred_element_type=jnp.float32
    )
    grad_key = jnp.einsum("td,te->de", input_one, grad_key_low, preferred_element_type=jnp.float32)
    grad_value = jnp.einsum(
        "td,te->de", input_one, grad_value_low, preferred_element_type=jnp.float32
    )
    grad_input_one = jnp.einsum(
        "te,de->td", grad_query_low, back_query, preferred_element_type=jnp.float32
    )
    grad_input_one = grad_input_one + jnp.einsum(
        "te,de->td", grad_key_low, back_key, preferred_element_type=jnp.float32
    )
    grad_input_one = grad_input_one + jnp.einsum(
        "te,de->td", grad_value_low, back_value, preferred_element_type=jnp.float32
    )
    grad_gain_one = jnp.sum(grad_input_one * normed_one, axis=0)
    grad_tokens = grad_middle + norm_backward(grad_input_one, normed_one, root_one, back_first)
    grad_gains = jnp.concatenate(
        [grad_gain_one, grad_gain_two, jnp.zeros((gain_length - 2 * D,), jnp.float32)]
    )
    shares = (
        lax.psum_scatter(grad_query.reshape(-1), "fsdp", scatter_dimension=0, tiled=True),
        lax.psum_scatter(grad_key.reshape(-1), "fsdp", scatter_dimension=0, tiled=True),
        lax.psum_scatter(grad_value.reshape(-1), "fsdp", scatter_dimension=0, tiled=True),
        lax.psum_scatter(grad_output.reshape(-1), "fsdp", scatter_dimension=0, tiled=True),
        lax.psum_scatter(grad_gate.reshape(-1), "fsdp", scatter_dimension=0, tiled=True),
        lax.psum_scatter(grad_up.reshape(-1), "fsdp", scatter_dimension=0, tiled=True),
        lax.psum_scatter(grad_down.reshape(-1), "fsdp", scatter_dimension=0, tiled=True),
        lax.psum_scatter(grad_gains, "fsdp", scatter_dimension=0, tiled=True),
    )
    return (
        output_tokens,
        grad_tokens.astype(jnp.bfloat16),
        shares[0],
        shares[1],
        shares[2],
        shares[3],
        shares[4],
        shares[5],
        shares[6],
        shares[7],
    )


AXIS_SIZES = (4, 2, 2, 2)
ORDERS = ((1, 0, 2), (0, 2, 1), (2, 0, 1), (0, 1, 2))
ARRAYS = 4
WIDE = 1536
NARROW = 640
SHAPES = ((16, WIDE), (16, WIDE), (16, WIDE), (64, NARROW))
MESH = pl.DeviceIdType.MESH


def coordinates():
    me = lax.axis_index("fsdp")
    return [me // 8, (me // 4) % 2, (me // 2) % 2, me % 2]


def device_at(coords):
    return ((coords[0] * 2 + coords[1]) * 2 + coords[2]) * 2 + coords[3]


def peers_along(coords, dim):
    found = []
    for offset in range(1, AXIS_SIZES[dim]):
        other = list(coords)
        other[dim] = lax.rem(coords[dim] + offset, AXIS_SIZES[dim])
        found.append(other)
    return found


def enter(coords):
    barrier = pltpu.get_barrier_semaphore()
    count = 0
    for dim in range(4):
        for other in peers_along(coords, dim):
            pl.semaphore_signal(barrier, inc=1, device_id=(device_at(other),), device_id_type=MESH)
            count += 1
    pl.semaphore_wait(barrier, count)


def gather_kernel(*refs):
    ins, outs = refs[:ARRAYS], refs[ARRAYS : 2 * ARRAYS]
    send_sem, recv_sem = refs[2 * ARRAYS :]
    coords = coordinates()
    enter(coords)

    def run(which):
        out = outs[which]
        out[coords[0], coords[1], coords[2], coords[3]] = ins[which][...]
        counter = [0]
        index = list(coords)
        sibling = peers_along(coords, 3)[0]
        core_copies = []

        def push(block, target):
            slot = counter[0]
            counter[0] += 1
            view = out.at[tuple(block)]
            copy = pltpu.make_async_remote_copy(
                src_ref=view,
                dst_ref=view,
                send_sem=send_sem.at[which, slot],
                recv_sem=recv_sem.at[which, slot],
                device_id=(device_at(target),),
                device_id_type=MESH,
            )
            copy.start()
            return copy

        pending_core = [list(index)]
        for dim in ORDERS[which]:
            copies = [push(index, other) for other in peers_along(coords, dim)]
            for block in pending_core:
                core_copies.append(push(block, sibling))
            pending_core = []
            yield
            for offset, copy in enumerate(copies):
                copy.wait()
                block = list(index)
                size = AXIS_SIZES[dim]
                block[dim] = lax.rem(coords[dim] + size - offset - 1, size)
                pending_core.append(block)
            index[dim] = slice(None)
        for block in pending_core:
            core_copies.append(push(block, sibling))
        yield
        for copy in core_copies:
            copy.wait()

    drive([run(which) for which in range(ARRAYS)])


def drive(tasks):
    while tasks:
        kept = []
        for task in tasks:
            try:
                next(task)
                kept.append(task)
            except StopIteration:
                pass
        tasks = kept


def scatter_kernel(*refs):
    ins, outs = refs[:ARRAYS], refs[ARRAYS : 2 * ARRAYS]
    landing = refs[2 * ARRAYS : 6 * ARRAYS]
    send_sem, recv_sem = refs[6 * ARRAYS :]
    coords = coordinates()
    enter(coords)

    def run(which):
        order = (3,) + tuple(reversed(ORDERS[which]))
        remaining = [0, 1, 2, 3]
        current = ins[which]
        counter = [0]

        def push(stage, dim, part, offset, target):
            slot = counter[0]
            counter[0] += 1
            index = tuple(
                part if axis == dim else slice(None) for axis in remaining
            )
            land = landing[which * 4 + stage]
            copy = pltpu.make_async_remote_copy(
                src_ref=current.at[index],
                dst_ref=land.at[offset],
                send_sem=send_sem.at[which, slot],
                recv_sem=recv_sem.at[which, slot],
                device_id=(device_at(target),),
                device_id_type=MESH,
            )
            copy.start()
            return copy

        copies = [
            push(0, 3, other[3], offset, other)
            for offset, other in enumerate(peers_along(coords, 3))
        ]
        for stage, dim in enumerate(order):
            yield
            for copy in copies:
                copy.wait()
            land = landing[which * 4 + stage]
            rest = [axis for axis in remaining if axis != dim]
            last = stage == 3

            def add_group(fixed, current=current, land=land, rest=rest, dim=dim, last=last, held=tuple(remaining)):
                loose = [axis for axis in rest if axis not in fixed]
                total = 1
                for axis in loose:
                    total *= AXIS_SIZES[axis]

                def body(step, carry):
                    at = dict(fixed)
                    left = step
                    for axis in reversed(loose):
                        at[axis] = left % AXIS_SIZES[axis]
                        left = left // AXIS_SIZES[axis]
                    mine = tuple(coords[dim] if axis == dim else at[axis] for axis in held)
                    target = tuple(at[axis] for axis in rest)
                    value = current[mine].astype(jnp.float32)
                    for offset in range(AXIS_SIZES[dim] - 1):
                        value = value + land[(offset,) + target].astype(jnp.float32)
                    if last:
                        outs[which][...] = value
                    else:
                        land[(0,) + target] = value.astype(jnp.bfloat16)
                    return carry

                if total == 1:
                    body(0, 0)
                else:
                    lax.fori_loop(0, total, body, 0)

            if last:
                add_group({})
                break
            following = order[stage + 1]
            remaining = rest
            current = land.at[0]
            copies = []
            for offset, other in enumerate(peers_along(coords, following)):
                add_group({following: other[following]})
                copies.append(push(stage + 1, following, other[following], offset, other))
            add_group({following: coords[following]})

    drive([run(which) for which in range(ARRAYS)])


def gather_packed(parts):
    return pl.pallas_call(
        gather_kernel,
        out_shape=tuple(jax.ShapeDtypeStruct(AXIS_SIZES + shape, jnp.bfloat16) for shape in SHAPES),
        in_specs=[pl.BlockSpec(memory_space=pltpu.VMEM)] * ARRAYS,
        out_specs=tuple([pl.BlockSpec(memory_space=pltpu.VMEM)] * ARRAYS),
        scratch_shapes=[
            pltpu.SemaphoreType.DMA((ARRAYS, 12)),
            pltpu.SemaphoreType.DMA((ARRAYS, 12)),
        ],
        compiler_params=pltpu.CompilerParams(
            collective_id=0, has_side_effects=True, vmem_limit_bytes=32 * 1024 * 1024
        ),
        name="gather_weights",
    )(*parts)


def scatter_packed(parts):
    landing = []
    for which in range(ARRAYS):
        remaining = [0, 1, 2, 3]
        for dim in (3,) + tuple(reversed(ORDERS[which])):
            remaining = [axis for axis in remaining if axis != dim]
            extent = tuple(AXIS_SIZES[axis] for axis in remaining)
            landing.append(
                pltpu.VMEM((AXIS_SIZES[dim] - 1,) + extent + SHAPES[which], jnp.bfloat16)
            )
    return pl.pallas_call(
        scatter_kernel,
        out_shape=tuple(jax.ShapeDtypeStruct(shape, jnp.float32) for shape in SHAPES),
        in_specs=[pl.BlockSpec(memory_space=pltpu.VMEM)] * ARRAYS,
        out_specs=tuple([pl.BlockSpec(memory_space=pltpu.VMEM)] * ARRAYS),
        scratch_shapes=landing
        + [
            pltpu.SemaphoreType.DMA((ARRAYS, 8)),
            pltpu.SemaphoreType.DMA((ARRAYS, 8)),
        ],
        compiler_params=pltpu.CompilerParams(
            collective_id=1, has_side_effects=True, vmem_limit_bytes=40 * 1024 * 1024
        ),
        name="scatter_gradients",
    )(*parts)


DEVICES = 32
ROWS = D // DEVICES
DOWN_ROWS = FF // DEVICES
SPILL = ROWS - 16


def order_matrix():
    true_index = np.concatenate(
        [
            (np.arange(DEVICES)[:, None] * ROWS + np.arange(16)[None, :]).reshape(-1),
            (np.arange(DEVICES)[:, None] * ROWS + 16 + np.arange(SPILL)[None, :]).reshape(-1),
        ]
    )
    matrix = np.zeros((D, D), np.float32)
    matrix[true_index, np.arange(D)] = 1.0
    return matrix.astype(ml_dtypes.bfloat16)


def dot(left, right, contract=(1, 0), precision=None):
    return lax.dot_general(
        left,
        right,
        (((contract[0],), (contract[1],)), ((), ())),
        preferred_element_type=jnp.float32,
        precision=precision,
    )


def low_dot(left, right, contract=(1, 0)):
    return dot(left, right, contract).astype(jnp.bfloat16)


def packed_device(
    tokens, segments, w_query, w_key, w_value, w_output, w_gate, w_up, w_down, gains, cotangent
):
    token_count = tokens.shape[0]
    group_size = HEADS // KV_HEADS
    score_scale = HEAD_DIM ** (-0.5)
    order = jnp.asarray(order_matrix())
    rows = jnp.concatenate(
        [
            w_query.reshape(ROWS, D),
            w_key.reshape(ROWS, KV),
            w_value.reshape(ROWS, KV),
            low_dot(w_output.reshape(ROWS, D), order),
            w_gate.reshape(ROWS, FF),
            w_up.reshape(ROWS, FF),
        ],
        axis=1,
    )
    down_rows = low_dot(w_down.reshape(DOWN_ROWS, D), order)
    share = gains.shape[0]
    spare = jnp.pad(gains.reshape(1, share), ((0, 63), (0, 64 - share)))
    extra = jnp.concatenate(
        [jnp.concatenate([rows[16:].reshape(16, D), down_rows], axis=0), spare], axis=1
    )
    mixed, gate_part, up_part, extra_all = gather_packed(
        (rows[:16, :WIDE], rows[:16, WIDE : 2 * WIDE], rows[:16, 2 * WIDE :], extra)
    )
    extra_all = extra_all.reshape(DEVICES, 64, NARROW)
    spill = extra_all[:, :16, :D].reshape(DEVICES * SPILL, 3 * WIDE)
    mixed = jnp.concatenate([mixed.reshape(512, WIDE), spill[:, :WIDE]], axis=0)
    gate_matrix = jnp.concatenate([gate_part.reshape(512, WIDE), spill[:, WIDE : 2 * WIDE]], axis=0)
    up_matrix = jnp.concatenate([up_part.reshape(512, WIDE), spill[:, 2 * WIDE :]], axis=0)
    down_matrix = extra_all[:, 16:, :D].reshape(FF, D)
    gain_all = extra_all[:, 0, D : D + share].reshape(2, D)
    gain_rows = dot(gain_all, order)
    gain_first, gain_second = gain_rows[0:1], gain_rows[1:2]
    qkv_matrix = mixed[:, : D + 2 * KV]
    output_matrix = mixed[:, D + 2 * KV :]

    column = jnp.arange(token_count)[None, :]
    row_index = jnp.arange(token_count)[:, None]
    same_segment = segments[:, None] == segments[None, :]
    positions = jnp.sum((same_segment & (column < row_index)).astype(jnp.int32), axis=1)
    allowed = same_segment & (column <= row_index)
    frequency = ROPE_BASE ** (-(2.0 * jnp.arange(HEAD_DIM // 2).astype(jnp.float32)) / HEAD_DIM)
    angles = positions.astype(jnp.float32)[:, None] * frequency[None, :]
    cosine = jnp.cos(angles)[:, None, :]
    sine_table = jnp.sin(angles)[:, None, :]
    live_rows = (segments >= 0).astype(jnp.float32)[:, None]

    token_values = dot(tokens, order)
    grad_result = dot(cotangent, order) * live_rows
    grad_down_in = grad_result.astype(jnp.bfloat16)

    normed_one, root_one = normalize_parts(token_values)
    input_one = (normed_one * gain_first).astype(jnp.bfloat16)
    qkv = dot(input_one, qkv_matrix)
    query_pre, key_pre = qkv[:, :D], qkv[:, D : D + KV]
    value_low = qkv[:, D + KV :].astype(jnp.bfloat16).reshape(token_count, KV_HEADS, HEAD_DIM)
    query_low = rotate(query_pre.reshape(token_count, HEADS, HEAD_DIM), cosine, sine_table).astype(
        jnp.bfloat16
    )
    query_low = query_low.reshape(token_count, KV_HEADS, group_size, HEAD_DIM)
    key_low = rotate(key_pre.reshape(token_count, KV_HEADS, HEAD_DIM), cosine, sine_table).astype(
        jnp.bfloat16
    )
    scores = (
        jnp.einsum("qkgd,tkd->kgqt", query_low, key_low, preferred_element_type=jnp.float32)
        * score_scale
    )
    scores = jnp.where(allowed, scores, NEG_LARGE)
    row_peak = jnp.max(scores, axis=-1, keepdims=True)
    exponentials = jnp.exp(scores - row_peak)
    totals = jnp.sum(exponentials, axis=-1, keepdims=True)
    probabilities = exponentials / totals
    probs_low = probabilities.astype(jnp.bfloat16)
    attended = jnp.einsum("kgqt,tkd->qkgd", probs_low, value_low, preferred_element_type=jnp.float32)
    attended_low = low_dot(attended.astype(jnp.bfloat16).reshape(token_count, D), order)
    middle = token_values + dot(attended_low, output_matrix)
    normed_two, root_two = normalize_parts(middle)
    input_two = (normed_two * gain_second).astype(jnp.bfloat16)
    gate_pre = dot(input_two, gate_matrix)
    up_pre = dot(input_two, up_matrix)
    sigmoid_gate = jax.nn.sigmoid(gate_pre)
    silu_gate = gate_pre * sigmoid_gate
    product_low = (silu_gate * up_pre).astype(jnp.bfloat16)
    result = middle + dot(product_low, down_matrix)
    output_tokens = low_dot((result * live_rows).astype(jnp.bfloat16), order, (1, 1))

    grad_down = low_dot(product_low, grad_down_in, (0, 0))
    grad_product = dot(grad_down_in, down_matrix, (1, 1))
    grad_gate_pre = (
        grad_product * up_pre * sigmoid_gate * (1.0 + gate_pre * (1.0 - sigmoid_gate))
    ).astype(jnp.bfloat16)
    grad_up_pre = (grad_product * silu_gate).astype(jnp.bfloat16)
    grad_gate = low_dot(input_two, grad_gate_pre, (0, 0))
    grad_up = low_dot(input_two, grad_up_pre, (0, 0))
    grad_input_two = dot(grad_gate_pre, gate_matrix, (1, 1)) + dot(grad_up_pre, up_matrix, (1, 1))
    grad_gain_two = jnp.sum(grad_input_two * normed_two, axis=0)
    grad_middle = grad_result + norm_backward(grad_input_two, normed_two, root_two, gain_second)
    grad_branch = grad_middle.astype(jnp.bfloat16)
    grad_output = low_dot(attended_low, grad_branch, (0, 0))
    grad_attended = low_dot(low_dot(grad_branch, output_matrix, (1, 1)), order, (1, 1))
    grad_attended = grad_attended.reshape(token_count, KV_HEADS, group_size, HEAD_DIM)

    grad_probs = jnp.einsum(
        "qkgd,tkd->kgqt", grad_attended, value_low, preferred_element_type=jnp.float32
    )
    centre = jnp.sum(probabilities * grad_probs, axis=-1, keepdims=True)
    grad_scores = (probabilities * (grad_probs - centre)).astype(jnp.bfloat16)
    grad_queries = (
        jnp.einsum("kgqt,tkd->qkgd", grad_scores, key_low, preferred_element_type=jnp.float32)
        * score_scale
    )
    grad_keys = (
        jnp.einsum("kgqt,qkgd->tkd", grad_scores, query_low, preferred_element_type=jnp.float32)
        * score_scale
    )
    grad_values = jnp.einsum(
        "kgqt,qkgd->tkd", probs_low, grad_attended, preferred_element_type=jnp.float32
    )
    grad_query_low = rotate_back(
        grad_queries.reshape(token_count, HEADS, HEAD_DIM), cosine, sine_table
    )
    grad_qkv = jnp.concatenate(
        [
            grad_query_low.astype(jnp.bfloat16).reshape(token_count, D),
            rotate_back(grad_keys, cosine, sine_table).astype(jnp.bfloat16).reshape(token_count, KV),
            grad_values.astype(jnp.bfloat16).reshape(token_count, KV),
        ],
        axis=1,
    )
    grad_mixed = jnp.concatenate([low_dot(input_one, grad_qkv, (0, 0)), grad_output], axis=1)
    grad_input_one = dot(grad_qkv, qkv_matrix, (1, 1))
    grad_gain_one = jnp.sum(grad_input_one * normed_one, axis=0)
    grad_tokens = grad_middle + norm_backward(grad_input_one, normed_one, root_one, gain_first)
    grad_tokens = low_dot(grad_tokens.astype(jnp.bfloat16), order, (1, 1))

    grad_gains = low_dot(jnp.stack([grad_gain_one, grad_gain_two]).astype(jnp.bfloat16), order, (1, 1))
    grad_gains = jnp.pad(
        grad_gains.reshape(DEVICES, 1, share), ((0, 0), (0, 63), (0, 64 - share))
    )
    spill = jnp.concatenate([grad_mixed[512:], grad_gate[512:], grad_up[512:]], axis=1)
    extra = jnp.concatenate(
        [spill.reshape(DEVICES, 16, D), grad_down.reshape(DEVICES, DOWN_ROWS, D)], axis=1
    )
    extra = jnp.concatenate([extra, grad_gains], axis=2)
    mixed, gate_part, up_part, extra = scatter_packed(
        (
            grad_mixed[:512].reshape(AXIS_SIZES + SHAPES[0]),
            grad_gate[:512].reshape(AXIS_SIZES + SHAPES[1]),
            grad_up[:512].reshape(AXIS_SIZES + SHAPES[2]),
            extra.reshape(AXIS_SIZES + SHAPES[3]),
        )
    )
    spill = extra[:16, :D].reshape(SPILL, 3 * WIDE)
    mixed = jnp.concatenate([mixed, spill[:, :WIDE]], axis=0)
    exact = lax.Precision.HIGHEST
    wide_order = order.astype(jnp.float32)
    return (
        output_tokens,
        grad_tokens,
        mixed[:, :D].reshape(-1),
        mixed[:, D : D + KV].reshape(-1),
        mixed[:, D + KV : D + 2 * KV].reshape(-1),
        dot(mixed[:, D + 2 * KV :], wide_order, (1, 1), exact).reshape(-1),
        jnp.concatenate([gate_part, spill[:, WIDE : 2 * WIDE]], axis=0).reshape(-1),
        jnp.concatenate([up_part, spill[:, 2 * WIDE :]], axis=0).reshape(-1),
        dot(extra[16:, :D], wide_order, (1, 1), exact).reshape(-1),
        extra[0, D : D + share],
    )


def solution(mesh):
    placed = (
        P("fsdp", None),
        P("fsdp"),
        P("fsdp"),
        P("fsdp"),
        P("fsdp"),
        P("fsdp"),
        P("fsdp"),
        P("fsdp"),
        P("fsdp"),
        P("fsdp"),
        P("fsdp", None),
    )
    return jax.shard_map(
        packed_device if mesh.shape["fsdp"] == DEVICES else per_device,
        mesh=mesh,
        in_specs=placed,
        out_specs=(
            P("fsdp", None),
            P("fsdp", None),
            P("fsdp"),
            P("fsdp"),
            P("fsdp"),
            P("fsdp"),
            P("fsdp"),
            P("fsdp"),
            P("fsdp"),
            P("fsdp"),
        ),
        check_vma=False,
    )
```

```python
import jax
import jax.numpy as jnp
import ml_dtypes
import numpy as np
from jax import lax
from jax.experimental import pallas as pl
from jax.experimental.pallas import tpu as pltpu
from jax.sharding import PartitionSpec as P

HEADS = 9
KV_HEADS = 3
HEAD_DIM = 64
FF = 1536
D = 576
KV = 192


ROPE_BASE = 100000.0
NORM_EPSILON = 1e-05
NEG_LARGE = -1e30


def unpack(flat_arrays):
    return (
        flat_arrays[0].reshape(D, D),
        flat_arrays[1].reshape(D, KV),
        flat_arrays[2].reshape(D, KV),
        flat_arrays[3].reshape(D, D),
        flat_arrays[4].reshape(D, FF),
        flat_arrays[5].reshape(D, FF),
        flat_arrays[6].reshape(FF, D),
        flat_arrays[7][:D].astype(jnp.float32),
        flat_arrays[7][D : 2 * D].astype(jnp.float32),
    )


def normalize_parts(values):
    inverse_root = lax.rsqrt(jnp.mean(values * values, axis=-1, keepdims=True) + NORM_EPSILON)
    return (values * inverse_root, inverse_root)


def norm_backward(grad_in, normed, inverse_root, gain_row):
    scaled = grad_in * gain_row
    return inverse_root * (scaled - normed * jnp.mean(scaled * normed, axis=-1, keepdims=True))


def rotate(values, cosine, sine_table):
    half_dim = values.shape[-1] // 2
    first_half = values[..., :half_dim]
    second_half = values[..., half_dim:]
    return jnp.concatenate(
        [
            first_half * cosine - second_half * sine_table,
            second_half * cosine + first_half * sine_table,
        ],
        axis=-1,
    )


def rotate_back(values, cosine, sine_table):
    half_dim = values.shape[-1] // 2
    first_half = values[..., :half_dim]
    second_half = values[..., half_dim:]
    return jnp.concatenate(
        [
            first_half * cosine + second_half * sine_table,
            second_half * cosine - first_half * sine_table,
        ],
        axis=-1,
    )


def per_device(
    tokens, segments, w_query, w_key, w_value, w_output, w_gate, w_up, w_down, gains, cotangent
):
    token_count = tokens.shape[0]
    group_size = HEADS // KV_HEADS
    score_scale = HEAD_DIM ** (-0.5)
    gain_length = gains.shape[0] * lax.axis_size("fsdp")
    gathered = (
        lax.all_gather(w_query, "fsdp", axis=0, tiled=True),
        lax.all_gather(w_key, "fsdp", axis=0, tiled=True),
        lax.all_gather(w_value, "fsdp", axis=0, tiled=True),
        lax.all_gather(w_output, "fsdp", axis=0, tiled=True),
        lax.all_gather(w_gate, "fsdp", axis=0, tiled=True),
        lax.all_gather(w_up, "fsdp", axis=0, tiled=True),
        lax.all_gather(w_down, "fsdp", axis=0, tiled=True),
        lax.all_gather(gains, "fsdp", axis=0, tiled=True),
    )
    (
        query_matrix,
        key_matrix,
        value_matrix,
        output_matrix,
        gate_matrix,
        up_matrix,
        down_matrix,
        gain_first,
        gain_second,
    ) = unpack(gathered)
    column = jnp.arange(token_count)[None, :]
    row_index = jnp.arange(token_count)[:, None]
    same_segment = segments[:, None] == segments[None, :]
    positions = jnp.sum((same_segment & (column < row_index)).astype(jnp.int32), axis=1)
    allowed = same_segment & (column <= row_index)
    frequency = ROPE_BASE ** (-(2.0 * jnp.arange(HEAD_DIM // 2).astype(jnp.float32)) / HEAD_DIM)
    angles = positions.astype(jnp.float32)[:, None] * frequency[None, :]
    cosine = jnp.cos(angles)[:, None, :]
    sine_table = jnp.sin(angles)[:, None, :]
    live_rows = (segments >= 0).astype(jnp.float32)[:, None]
    token_values = tokens.astype(jnp.float32)
    normed_one, root_one = normalize_parts(token_values)
    input_one = (normed_one * gain_first).astype(jnp.bfloat16)
    query_pre = jnp.dot(input_one, query_matrix, preferred_element_type=jnp.float32)
    key_pre = jnp.dot(input_one, key_matrix, preferred_element_type=jnp.float32)
    value_low = jnp.dot(input_one, value_matrix, preferred_element_type=jnp.float32).astype(
        jnp.bfloat16
    )
    value_low = value_low.reshape(token_count, KV_HEADS, HEAD_DIM)
    query_low = rotate(query_pre.reshape(token_count, HEADS, HEAD_DIM), cosine, sine_table).astype(
        jnp.bfloat16
    )
    query_low = query_low.reshape(token_count, KV_HEADS, group_size, HEAD_DIM)
    key_low = rotate(key_pre.reshape(token_count, KV_HEADS, HEAD_DIM), cosine, sine_table).astype(
        jnp.bfloat16
    )
    block_rows = min(token_count, 512)
    block_count = token_count // block_rows

    def masked_scores():
        scores = (
            jnp.einsum("qkgd,tkd->kgqt", query_low, key_low, preferred_element_type=jnp.float32)
            * score_scale
        )
        return (query_low, jnp.where(allowed, scores, NEG_LARGE))

    def attend(block_index):
        query_block, scores = masked_scores()
        row_peak = jnp.max(scores, axis=-1, keepdims=True)
        exponentials = jnp.exp(scores - row_peak)
        totals = jnp.sum(exponentials, axis=-1, keepdims=True)
        probabilities = (exponentials / totals).astype(jnp.bfloat16)
        attended = jnp.einsum(
            "kgqt,tkd->qkgd", probabilities, value_low, preferred_element_type=jnp.float32
        )
        return (attended.astype(jnp.bfloat16), row_peak[..., 0] + jnp.log(totals[..., 0]))

    attended_blocks, log_totals = lax.map(attend, jnp.arange(block_count))
    attended_low = attended_blocks.reshape(token_count, D)
    branch = jnp.dot(attended_low, output_matrix, preferred_element_type=jnp.float32)
    middle = token_values + branch
    normed_two, root_two = normalize_parts(middle)
    input_two = (normed_two * gain_second).astype(jnp.bfloat16)
    gate_pre = jnp.dot(input_two, gate_matrix, preferred_element_type=jnp.float32)
    up_pre = jnp.dot(input_two, up_matrix, preferred_element_type=jnp.float32)
    sigmoid_gate = jax.nn.sigmoid(gate_pre)
    silu_gate = gate_pre * sigmoid_gate
    product_low = (silu_gate * up_pre).astype(jnp.bfloat16)
    result = middle + jnp.dot(product_low, down_matrix, preferred_element_type=jnp.float32)
    output_tokens = (result * live_rows).astype(jnp.bfloat16)
    regathered = (
        lax.all_gather(w_query, "fsdp", axis=0, tiled=True),
        lax.all_gather(w_key, "fsdp", axis=0, tiled=True),
        lax.all_gather(w_value, "fsdp", axis=0, tiled=True),
        lax.all_gather(w_output, "fsdp", axis=0, tiled=True),
        lax.all_gather(w_gate, "fsdp", axis=0, tiled=True),
        lax.all_gather(w_up, "fsdp", axis=0, tiled=True),
        lax.all_gather(w_down, "fsdp", axis=0, tiled=True),
        lax.all_gather(gains, "fsdp", axis=0, tiled=True),
    )
    back_weights = unpack(regathered)
    (
        back_query,
        back_key,
        back_value,
        back_output,
        back_gate,
        back_up,
        back_down,
        back_first,
        back_second,
    ) = back_weights
    grad_result = cotangent.astype(jnp.float32) * live_rows
    grad_down_in = grad_result.astype(jnp.bfloat16)
    grad_down = jnp.einsum(
        "tf,td->fd", product_low, grad_down_in, preferred_element_type=jnp.float32
    )
    grad_product = jnp.einsum(
        "td,fd->tf", grad_down_in, back_down, preferred_element_type=jnp.float32
    )
    grad_gate_pre = (
        grad_product * up_pre * sigmoid_gate * (1.0 + gate_pre * (1.0 - sigmoid_gate))
    ).astype(jnp.bfloat16)
    grad_up_pre = (grad_product * silu_gate).astype(jnp.bfloat16)
    grad_gate = jnp.einsum(
        "td,tf->df", input_two, grad_gate_pre, preferred_element_type=jnp.float32
    )
    grad_up = jnp.einsum("td,tf->df", input_two, grad_up_pre, preferred_element_type=jnp.float32)
    grad_input_two = jnp.einsum(
        "tf,df->td", grad_gate_pre, back_gate, preferred_element_type=jnp.float32
    )
    grad_input_two = grad_input_two + jnp.einsum(
        "tf,df->td", grad_up_pre, back_up, preferred_element_type=jnp.float32
    )
    grad_gain_two = jnp.sum(grad_input_two * normed_two, axis=0)
    grad_middle = grad_result + norm_backward(grad_input_two, normed_two, root_two, back_second)
    grad_branch = grad_middle.astype(jnp.bfloat16)
    grad_output = jnp.einsum(
        "td,te->de", attended_low, grad_branch, preferred_element_type=jnp.float32
    )
    grad_attended = jnp.einsum(
        "te,de->td", grad_branch, back_output, preferred_element_type=jnp.float32
    ).astype(jnp.bfloat16)
    grad_attended = grad_attended.reshape(token_count, KV_HEADS, group_size, HEAD_DIM)

    def back_step(carried, inputs):
        grad_keys, grad_values = carried
        block_index, log_block = inputs
        query_block, scores = masked_scores()
        probabilities = jnp.exp(scores - log_block[..., None])
        grad_probs = jnp.einsum(
            "qkgd,tkd->kgqt", grad_attended, value_low, preferred_element_type=jnp.float32
        )
        centre = jnp.sum(probabilities * grad_probs, axis=-1, keepdims=True)
        grad_scores = (probabilities * (grad_probs - centre)).astype(jnp.bfloat16)
        grad_query_block = (
            jnp.einsum("kgqt,tkd->qkgd", grad_scores, key_low, preferred_element_type=jnp.float32)
            * score_scale
        )
        grad_keys = (
            grad_keys
            + jnp.einsum(
                "kgqt,qkgd->tkd", grad_scores, query_block, preferred_element_type=jnp.float32
            )
            * score_scale
        )
        grad_values = grad_values + jnp.einsum(
            "kgqt,qkgd->tkd",
            probabilities.astype(jnp.bfloat16),
            grad_attended,
            preferred_element_type=jnp.float32,
        )
        return ((grad_keys, grad_values), grad_query_block)

    zero_state = jnp.zeros((token_count, KV_HEADS, HEAD_DIM), jnp.float32)
    (grad_keys, grad_values), grad_query_blocks = lax.scan(
        back_step, (zero_state, zero_state), (jnp.arange(block_count), log_totals)
    )
    grad_query_low = rotate_back(
        grad_query_blocks.reshape(token_count, HEADS, HEAD_DIM), cosine, sine_table
    )
    grad_query_low = grad_query_low.astype(jnp.bfloat16).reshape(token_count, D)
    grad_key_low = (
        rotate_back(grad_keys, cosine, sine_table).astype(jnp.bfloat16).reshape(token_count, KV)
    )
    grad_value_low = grad_values.astype(jnp.bfloat16).reshape(token_count, KV)
    grad_query = jnp.einsum(
        "td,te->de", input_one, grad_query_low, preferred_element_type=jnp.float32
    )
    grad_key = jnp.einsum("td,te->de", input_one, grad_key_low, preferred_element_type=jnp.float32)
    grad_value = jnp.einsum(
        "td,te->de", input_one, grad_value_low, preferred_element_type=jnp.float32
    )
    grad_input_one = jnp.einsum(
        "te,de->td", grad_query_low, back_query, preferred_element_type=jnp.float32
    )
    grad_input_one = grad_input_one + jnp.einsum(
        "te,de->td", grad_key_low, back_key, preferred_element_type=jnp.float32
    )
    grad_input_one = grad_input_one + jnp.einsum(
        "te,de->td", grad_value_low, back_value, preferred_element_type=jnp.float32
    )
    grad_gain_one = jnp.sum(grad_input_one * normed_one, axis=0)
    grad_tokens = grad_middle + norm_backward(grad_input_one, normed_one, root_one, back_first)
    grad_gains = jnp.concatenate(
        [grad_gain_one, grad_gain_two, jnp.zeros((gain_length - 2 * D,), jnp.float32)]
    )
    shares = (
        lax.psum_scatter(grad_query.reshape(-1), "fsdp", scatter_dimension=0, tiled=True),
        lax.psum_scatter(grad_key.reshape(-1), "fsdp", scatter_dimension=0, tiled=True),
        lax.psum_scatter(grad_value.reshape(-1), "fsdp", scatter_dimension=0, tiled=True),
        lax.psum_scatter(grad_output.reshape(-1), "fsdp", scatter_dimension=0, tiled=True),
        lax.psum_scatter(grad_gate.reshape(-1), "fsdp", scatter_dimension=0, tiled=True),
        lax.psum_scatter(grad_up.reshape(-1), "fsdp", scatter_dimension=0, tiled=True),
        lax.psum_scatter(grad_down.reshape(-1), "fsdp", scatter_dimension=0, tiled=True),
        lax.psum_scatter(grad_gains, "fsdp", scatter_dimension=0, tiled=True),
    )
    return (
        output_tokens,
        grad_tokens.astype(jnp.bfloat16),
        shares[0],
        shares[1],
        shares[2],
        shares[3],
        shares[4],
        shares[5],
        shares[6],
        shares[7],
    )


AXIS_SIZES = (4, 2, 2, 2)
ORDERS = ((1, 0, 2), (0, 2, 1), (2, 0, 1), (0, 1, 2))
ARRAYS = 4
WIDE = 1536
NARROW = 640
SHAPES = ((16, WIDE), (16, WIDE), (16, WIDE), (64, NARROW))
MESH = pl.DeviceIdType.MESH


def coordinates():
    me = lax.axis_index("fsdp")
    return [me // 8, (me // 4) % 2, (me // 2) % 2, me % 2]


def device_at(coords):
    return ((coords[0] * 2 + coords[1]) * 2 + coords[2]) * 2 + coords[3]


def peers_along(coords, dim):
    found = []
    for offset in range(1, AXIS_SIZES[dim]):
        other = list(coords)
        other[dim] = lax.rem(coords[dim] + offset, AXIS_SIZES[dim])
        found.append(other)
    return found


def enter(coords):
    barrier = pltpu.get_barrier_semaphore()
    count = 0
    for dim in range(4):
        for other in peers_along(coords, dim):
            pl.semaphore_signal(barrier, inc=1, device_id=(device_at(other),), device_id_type=MESH)
            count += 1
    pl.semaphore_wait(barrier, count)


def gather_kernel(*refs):
    ins, outs = refs[:ARRAYS], refs[ARRAYS : 2 * ARRAYS]
    send_sem, recv_sem = refs[2 * ARRAYS :]
    coords = coordinates()
    enter(coords)

    def run(which):
        out = outs[which]
        out[coords[0], coords[1], coords[2], coords[3]] = ins[which][...]
        counter = [0]
        index = list(coords)
        sibling = peers_along(coords, 3)[0]
        core_copies = []

        def push(block, target):
            slot = counter[0]
            counter[0] += 1
            view = out.at[tuple(block)]
            copy = pltpu.make_async_remote_copy(
                src_ref=view,
                dst_ref=view,
                send_sem=send_sem.at[which, slot],
                recv_sem=recv_sem.at[which, slot],
                device_id=(device_at(target),),
                device_id_type=MESH,
            )
            copy.start()
            return copy

        pending_core = [list(index)]
        for dim in ORDERS[which]:
            copies = [push(index, other) for other in peers_along(coords, dim)]
            for block in pending_core:
                core_copies.append(push(block, sibling))
            pending_core = []
            yield
            for offset, copy in enumerate(copies):
                copy.wait()
                block = list(index)
                size = AXIS_SIZES[dim]
                block[dim] = lax.rem(coords[dim] + size - offset - 1, size)
                pending_core.append(block)
            index[dim] = slice(None)
        for block in pending_core:
            core_copies.append(push(block, sibling))
        yield
        for copy in core_copies:
            copy.wait()

    drive([run(which) for which in range(ARRAYS)])


def drive(tasks):
    while tasks:
        kept = []
        for task in tasks:
            try:
                next(task)
                kept.append(task)
            except StopIteration:
                pass
        tasks = kept


def scatter_kernel(*refs):
    ins, outs = refs[:ARRAYS], refs[ARRAYS : 2 * ARRAYS]
    landing = refs[2 * ARRAYS : 6 * ARRAYS]
    send_sem, recv_sem = refs[6 * ARRAYS :]
    coords = coordinates()
    enter(coords)

    def run(which):
        order = (3,) + tuple(reversed(ORDERS[which]))
        remaining = [0, 1, 2, 3]
        current = ins[which]
        counter = [0]

        def push(stage, dim, part, offset, target):
            slot = counter[0]
            counter[0] += 1
            index = tuple(
                part if axis == dim else slice(None) for axis in remaining
            )
            land = landing[which * 4 + stage]
            copy = pltpu.make_async_remote_copy(
                src_ref=current.at[index],
                dst_ref=land.at[offset],
                send_sem=send_sem.at[which, slot],
                recv_sem=recv_sem.at[which, slot],
                device_id=(device_at(target),),
                device_id_type=MESH,
            )
            copy.start()
            return copy

        copies = [
            push(0, 3, other[3], offset, other)
            for offset, other in enumerate(peers_along(coords, 3))
        ]
        for stage, dim in enumerate(order):
            yield
            for copy in copies:
                copy.wait()
            land = landing[which * 4 + stage]
            rest = [axis for axis in remaining if axis != dim]
            last = stage == 3

            def add_group(fixed, current=current, land=land, rest=rest, dim=dim, last=last, held=tuple(remaining)):
                loose = [axis for axis in rest if axis not in fixed]
                total = 1
                for axis in loose:
                    total *= AXIS_SIZES[axis]

                def body(step, carry):
                    at = dict(fixed)
                    left = step
                    for axis in reversed(loose):
                        at[axis] = left % AXIS_SIZES[axis]
                        left = left // AXIS_SIZES[axis]
                    mine = tuple(coords[dim] if axis == dim else at[axis] for axis in held)
                    target = tuple(at[axis] for axis in rest)
                    value = current[mine].astype(jnp.float32)
                    for offset in range(AXIS_SIZES[dim] - 1):
                        value = value + land[(offset,) + target].astype(jnp.float32)
                    if last:
                        outs[which][...] = value
                    else:
                        land[(0,) + target] = value.astype(jnp.bfloat16)
                    return carry

                if total == 1:
                    body(0, 0)
                else:
                    lax.fori_loop(0, total, body, 0)

            if last:
                add_group({})
                break
            following = order[stage + 1]
            remaining = rest
            current = land.at[0]
            copies = []
            for offset, other in enumerate(peers_along(coords, following)):
                add_group({following: other[following]})
                copies.append(push(stage + 1, following, other[following], offset, other))
            add_group({following: coords[following]})

    drive([run(which) for which in range(ARRAYS)])


def gather_packed(parts):
    return pl.pallas_call(
        gather_kernel,
        out_shape=tuple(jax.ShapeDtypeStruct(AXIS_SIZES + shape, jnp.bfloat16) for shape in SHAPES),
        in_specs=[pl.BlockSpec(memory_space=pltpu.VMEM)] * ARRAYS,
        out_specs=tuple([pl.BlockSpec(memory_space=pltpu.VMEM)] * ARRAYS),
        scratch_shapes=[
            pltpu.SemaphoreType.DMA((ARRAYS, 12)),
            pltpu.SemaphoreType.DMA((ARRAYS, 12)),
        ],
        compiler_params=pltpu.CompilerParams(
            collective_id=0, has_side_effects=True, vmem_limit_bytes=32 * 1024 * 1024
        ),
        name="gather_weights",
    )(*parts)


def scatter_packed(parts):
    landing = []
    for which in range(ARRAYS):
        remaining = [0, 1, 2, 3]
        for dim in (3,) + tuple(reversed(ORDERS[which])):
            remaining = [axis for axis in remaining if axis != dim]
            extent = tuple(AXIS_SIZES[axis] for axis in remaining)
            landing.append(
                pltpu.VMEM((AXIS_SIZES[dim] - 1,) + extent + SHAPES[which], jnp.bfloat16)
            )
    return pl.pallas_call(
        scatter_kernel,
        out_shape=tuple(jax.ShapeDtypeStruct(shape, jnp.float32) for shape in SHAPES),
        in_specs=[pl.BlockSpec(memory_space=pltpu.VMEM)] * ARRAYS,
        out_specs=tuple([pl.BlockSpec(memory_space=pltpu.VMEM)] * ARRAYS),
        scratch_shapes=landing
        + [
            pltpu.SemaphoreType.DMA((ARRAYS, 8)),
            pltpu.SemaphoreType.DMA((ARRAYS, 8)),
        ],
        compiler_params=pltpu.CompilerParams(
            collective_id=1, has_side_effects=True, vmem_limit_bytes=40 * 1024 * 1024
        ),
        name="scatter_gradients",
    )(*parts)


DEVICES = 32
ROWS = D // DEVICES
DOWN_ROWS = FF // DEVICES
SPILL = ROWS - 16


STREAM = 640
CHUNK = 512
PER_GAIN = 36


def order_matrices():
    main = (np.arange(DEVICES)[:, None] * ROWS + np.arange(16)[None, :]).reshape(-1)
    spill = (np.arange(DEVICES)[:, None] * ROWS + 16 + np.arange(SPILL)[None, :]).reshape(-1)
    stream = np.zeros((D, STREAM), np.float32)
    stream[main, np.arange(512)] = 1.0
    stream[spill, 576 + np.arange(64)] = 1.0
    columns = np.concatenate([stream[:, 576:], stream[:, :512]], axis=1)
    select = np.zeros((512, 512), np.float32)
    for part in range(8):
        for owner in range(DEVICES):
            for row in range(SPILL):
                select[part * 64 + owner * 2 + row, owner * 16 + row * 8 + part] = 1.0
    true_index = np.full((STREAM,), -1)
    true_index[:512] = main
    true_index[576:] = spill
    pick = np.zeros((2, 64, STREAM), np.float32)
    holder = np.zeros((2, 64, STREAM), np.float32)
    for half in range(2):
        for lane in range(STREAM):
            if true_index[lane] >= 0:
                flat = half * D + true_index[lane]
                pick[half, flat % PER_GAIN, lane] = 1.0
                holder[half, 2 * (flat // PER_GAIN), lane] = 1.0
    return tuple(value.astype(ml_dtypes.bfloat16) for value in (stream, columns, select, pick, holder))


def dot(left, right, contract=(1, 0), precision=None):
    return lax.dot_general(
        left,
        right,
        (((contract[0],), (contract[1],)), ((), ())),
        preferred_element_type=jnp.float32,
        precision=precision,
    )


def low_dot(left, right, contract=(1, 0)):
    return dot(left, right, contract).astype(jnp.bfloat16)


def swap_halves(values):
    width = values.shape[1]
    lane = lax.broadcasted_iota(jnp.int32, values.shape, 1)
    return jnp.where(
        lane % HEAD_DIM < HEAD_DIM // 2,
        pltpu.roll(values, width - HEAD_DIM // 2, 1),
        pltpu.roll(values, HEAD_DIM // 2, 1),
    )


def stream_norm(values):
    root = lax.rsqrt(jnp.sum(values * values, axis=1, keepdims=True) * (1.0 / D) + NORM_EPSILON)
    return values * root, root


def stream_norm_back(grad_in, normed, root, gain_row):
    scaled = grad_in * gain_row
    mean = jnp.sum(scaled * normed, axis=1, keepdims=True) * (1.0 / D)
    return root * (scaled - normed * mean)


def layer_kernel(
    tokens, cotangent, seg_row, seg_col, cosine, sine, stream, select, pick, holder,
    mixed, gate, up, extra,
    out_tokens, out_grad_tokens, g_mixed, g_gate, g_up, g_extra,
    w_spill, w_down, g_spill, probs, heads, attended, g_heads, result, g_input,
):
    low = jnp.bfloat16
    count = tokens.shape[0]
    scale = HEAD_DIM ** (-0.5)
    spill_in = extra[:, :16, :].reshape(512, STREAM)
    spill_rows = low_dot(select[...], spill_in)
    w_spill[0:64, :] = jnp.zeros((64, 8 * STREAM), low)
    for part in range(8):
        w_spill[64:128, part * STREAM : (part + 1) * STREAM] = spill_rows[part * 64 : part * 64 + 64]
    w_down[...] = extra[:, 16:, :].reshape(FF, STREAM)
    gain_block = spill_rows[448:512, 128:192]
    gains = [
        jnp.sum(dot(gain_block, pick[half]) * holder[half].astype(jnp.float32), axis=0, keepdims=True)
        for half in range(2)
    ]

    values = dot(tokens[...], stream[...])
    live = (seg_col[...] >= 0).astype(jnp.float32)
    grad_result = dot(cotangent[...], stream[...]) * live
    grad_down_in = grad_result.astype(low)
    normed_one, root_one = stream_norm(values)
    input_one = (normed_one * gains[0]).astype(low)
    one_main, one_spill = input_one[:, :512], input_one[:, 512:]
    qkv = dot(one_main, mixed[:, :1024]) + dot(one_spill, w_spill[:, :1024])
    wide_cos = jnp.concatenate([cosine[...]] * 6, axis=1)
    wide_sin = jnp.concatenate([sine[...]] * 6, axis=1)
    turning = qkv[:, :768]
    heads[:, :768] = (turning * wide_cos + swap_halves(turning) * wide_sin).astype(low)
    heads[:, 768:] = qkv[:, 768:].astype(low)
    column = lax.broadcasted_iota(jnp.int32, (count, count), 1)
    row = lax.broadcasted_iota(jnp.int32, (count, count), 0)
    allowed = (seg_col[...] == seg_row[...]) & (column <= row)

    def head(array, start):
        return array[:, start : start + HEAD_DIM]

    for h in range(HEADS):
        c = h // 3
        scores = dot(head(heads, 64 * h), head(heads, 576 + 64 * c), (1, 1)) * scale
        scores = jnp.where(allowed, scores, NEG_LARGE)
        peak = jnp.max(scores, axis=1, keepdims=True)
        powers = jnp.exp(scores - peak)
        p = powers / jnp.sum(powers, axis=1, keepdims=True)
        probs[h] = p
        attended[:, 64 * h : 64 * h + 64] = low_dot(p.astype(low), head(heads, 768 + 64 * c))
    att = low_dot(attended[...], stream[...])
    att_main, att_spill = att[:, :512], att[:, 512:]
    branch_main = dot(att_main, mixed[:, 1024:]) + dot(att_spill, w_spill[:, 1024:1536])
    branch_spill = dot(att_main, mixed[:, 896:1024]) + dot(att_spill, w_spill[:, 896:1024])
    lane = lax.broadcasted_iota(jnp.int32, branch_spill.shape, 1)
    branch_spill = jnp.where(lane >= 64, branch_spill, 0.0)
    middle = values + jnp.concatenate([branch_main, branch_spill], axis=1)
    normed_two, root_two = stream_norm(middle)
    input_two = (normed_two * gains[1]).astype(low)
    two_main, two_spill = input_two[:, :512], input_two[:, 512:]
    result[...] = middle
    g_input[...] = jnp.zeros_like(g_input)

    for start in range(0, FF, CHUNK):
        here = slice(start, start + CHUNK)
        gate_at = slice(FF + start, FF + start + CHUNK)
        up_at = slice(2 * FF + start, 2 * FF + start + CHUNK)
        gate_pre = dot(two_main, gate[:, here]) + dot(two_spill, w_spill[:, gate_at])
        up_pre = dot(two_main, up[:, here]) + dot(two_spill, w_spill[:, up_at])
        sig = 1.0 / (1.0 + jnp.exp(-gate_pre))
        silu = gate_pre * sig
        product = (silu * up_pre).astype(low)
        down = w_down[here, :]
        result[...] += dot(product, down)
        w_down_grad = low_dot(product, grad_down_in, (0, 0))
        g_product = dot(grad_down_in, down, (1, 1))
        gg = (g_product * up_pre * sig * (1.0 + gate_pre * (1.0 - sig))).astype(low)
        gu = (g_product * silu).astype(low)
        g_input[:, :512] += dot(gg, gate[:, here], (1, 1)) + dot(gu, up[:, here], (1, 1))
        g_input[:, 512:] += dot(gg, w_spill[:, gate_at], (1, 1)) + dot(gu, w_spill[:, up_at], (1, 1))
        g_gate[:, here] = low_dot(two_main, gg, (0, 0))
        g_up[:, here] = low_dot(two_main, gu, (0, 0))
        g_spill[:, gate_at] = low_dot(two_spill, gg, (0, 0))[64:]
        g_spill[:, up_at] = low_dot(two_spill, gu, (0, 0))[64:]
        w_down[here, :] = w_down_grad
    g_extra[:, 16:, :] = w_down[...].reshape(DEVICES, DOWN_ROWS, STREAM)
    out_tokens[...] = low_dot((result[...] * live).astype(low), stream[...], (1, 1))

    grad_input_two = g_input[...]
    gain_grads = [None, jnp.sum(grad_input_two * normed_two, axis=0, keepdims=True)]
    grad_middle = grad_result + stream_norm_back(grad_input_two, normed_two, root_two, gains[1])
    grad_branch = grad_middle.astype(low)
    branch_main, branch_spill = grad_branch[:, :512], grad_branch[:, 512:]
    g_mixed[:, 1024:] = low_dot(att_main, branch_main, (0, 0))
    g_spill[:, 1024:1536] = low_dot(att_spill, branch_main, (0, 0))[64:]
    g_att = jnp.concatenate(
        [
            dot(branch_main, mixed[:, 1024:], (1, 1)) + dot(branch_spill, mixed[:, 896:1024], (1, 1)),
            dot(branch_main, w_spill[:, 1024:1536], (1, 1))
            + dot(branch_spill, w_spill[:, 896:1024], (1, 1)),
        ],
        axis=1,
    )
    attended[...] = low_dot(g_att.astype(low), stream[...], (1, 1))
    g_heads[:, 896:] = jnp.zeros((count, 128), jnp.float32)
    for c in range(KV_HEADS):
        keys, vals = head(heads, 576 + 64 * c), head(heads, 768 + 64 * c)
        g_keys, g_vals = 0.0, 0.0
        for h in range(3 * c, 3 * c + 3):
            p, g_a, q = probs[h], head(attended, 64 * h), head(heads, 64 * h)
            gp = dot(g_a, vals, (1, 1))
            centre = jnp.sum(p * gp, axis=1, keepdims=True)
            gs = (p * (gp - centre)).astype(low)
            g_heads[:, 64 * h : 64 * h + 64] = dot(gs, keys) * scale
            g_keys = g_keys + dot(gs, q, (0, 0))
            g_vals = g_vals + dot(p.astype(low), g_a, (0, 0))
        g_heads[:, 576 + 64 * c : 640 + 64 * c] = g_keys * scale
        g_heads[:, 768 + 64 * c : 832 + 64 * c] = g_vals
    turning = g_heads[:, :768]
    grad_qkv = jnp.concatenate(
        [turning * wide_cos - swap_halves(turning) * wide_sin, g_heads[:, 768:]], axis=1
    ).astype(low)
    g_mixed[:, :896] = low_dot(one_main, grad_qkv[:, :896], (0, 0))
    g_spill[:, :896] = low_dot(one_spill, grad_qkv[:, :896], (0, 0))[64:]
    tail = grad_qkv[:, 896:]
    g_mixed[:, 896:1024] = (dot(one_main, tail, (0, 0)) + dot(att_main, branch_spill, (0, 0))).astype(low)
    g_spill[:, 896:1024] = (dot(one_spill, tail, (0, 0)) + dot(att_spill, branch_spill, (0, 0))).astype(low)[64:]
    grad_input_one = jnp.concatenate(
        [dot(grad_qkv, mixed[:, :1024], (1, 1)), dot(grad_qkv, w_spill[:, :1024], (1, 1))], axis=1
    )
    gain_grads[0] = jnp.sum(grad_input_one * normed_one, axis=0, keepdims=True)
    grad_tokens = grad_middle + stream_norm_back(grad_input_one, normed_one, root_one, gains[0])
    out_grad_tokens[...] = low_dot(grad_tokens.astype(low), stream[...], (1, 1))
    block = 0.0
    for half in range(2):
        spread = holder[half].astype(jnp.float32) * gain_grads[half]
        block = block + dot(spread.astype(low), pick[half], (1, 1))
    g_spill[:, 3 * FF :] = jnp.concatenate(
        [block, jnp.zeros((64, 8 * STREAM - 3 * FF - 64), jnp.float32)], axis=1
    ).astype(low)
    stacked = jnp.concatenate(
        [g_spill[:, part * STREAM : (part + 1) * STREAM] for part in range(8)], axis=0
    )
    g_extra[:, :16, :] = low_dot(select[...], stacked, (0, 0)).reshape(DEVICES, 16, STREAM)


def local_layer(*operands):
    count = operands[0].shape[0]
    low = jnp.bfloat16
    vmem = pl.BlockSpec(memory_space=pltpu.VMEM)
    return pl.pallas_call(
        layer_kernel,
        out_shape=(
            jax.ShapeDtypeStruct((count, D), low),
            jax.ShapeDtypeStruct((count, D), low),
            jax.ShapeDtypeStruct((512, WIDE), low),
            jax.ShapeDtypeStruct((512, WIDE), low),
            jax.ShapeDtypeStruct((512, WIDE), low),
            jax.ShapeDtypeStruct((DEVICES, 64, STREAM), low),
        ),
        in_specs=[vmem] * len(operands),
        out_specs=(vmem,) * 6,
        scratch_shapes=[
            pltpu.VMEM((128, 8 * STREAM), low),
            pltpu.VMEM((FF, STREAM), low),
            pltpu.VMEM((64, 8 * STREAM), low),
            pltpu.VMEM((HEADS, count, count), jnp.float32),
            pltpu.VMEM((count, 1024), low),
            pltpu.VMEM((count, D), low),
            pltpu.VMEM((count, 1024), jnp.float32),
            pltpu.VMEM((count, STREAM), jnp.float32),
            pltpu.VMEM((count, STREAM), jnp.float32),
        ],
        compiler_params=pltpu.CompilerParams(vmem_limit_bytes=52 * 1024 * 1024),
        name="local_layer",
    )(*operands)


def packed_device(
    tokens, segments, w_query, w_key, w_value, w_output, w_gate, w_up, w_down, gains, cotangent
):
    token_count = tokens.shape[0]
    stream, columns, select, pick, holder = (jnp.asarray(value) for value in order_matrices())
    share = gains.shape[0]
    rows = jnp.concatenate(
        [
            w_query.reshape(ROWS, D),
            w_key.reshape(ROWS, KV),
            w_value.reshape(ROWS, KV),
            low_dot(w_output.reshape(ROWS, D), columns),
            w_gate.reshape(ROWS, FF),
            w_up.reshape(ROWS, FF),
        ],
        axis=1,
    )
    down_rows = low_dot(w_down.reshape(DOWN_ROWS, D), stream)
    spare = jnp.pad(gains.reshape(1, share), ((0, 1), (0, 8 * STREAM - 3 * FF - share)))
    spill = jnp.concatenate([rows[16:], spare], axis=1).reshape(16, STREAM)
    weights = gather_packed(
        (
            rows[:16, :WIDE],
            rows[:16, WIDE : 2 * WIDE],
            rows[:16, 2 * WIDE :],
            jnp.concatenate([spill, down_rows], axis=0),
        )
    )
    column = jnp.arange(token_count)[None, :]
    row_index = jnp.arange(token_count)[:, None]
    same_segment = segments[:, None] == segments[None, :]
    positions = jnp.sum((same_segment & (column < row_index)).astype(jnp.int32), axis=1)
    frequency = ROPE_BASE ** (-(2.0 * jnp.arange(HEAD_DIM // 2).astype(jnp.float32)) / HEAD_DIM)
    angles = positions.astype(jnp.float32)[:, None] * frequency[None, :]
    cosine, sine = jnp.cos(angles), jnp.sin(angles)
    output_tokens, grad_tokens, g_mixed, g_gate, g_up, g_extra = local_layer(
        tokens,
        cotangent,
        segments[None, :],
        segments[:, None],
        jnp.concatenate([cosine] * 4, axis=1),
        jnp.concatenate([-sine, sine, -sine, sine], axis=1),
        stream,
        select,
        pick,
        holder,
        weights[0].reshape(512, WIDE),
        weights[1].reshape(512, WIDE),
        weights[2].reshape(512, WIDE),
        weights[3].reshape(DEVICES, 64, STREAM),
    )
    mixed, gate_part, up_part, extra = scatter_packed(
        (
            g_mixed.reshape(AXIS_SIZES + SHAPES[0]),
            g_gate.reshape(AXIS_SIZES + SHAPES[1]),
            g_up.reshape(AXIS_SIZES + SHAPES[2]),
            g_extra.reshape(AXIS_SIZES + SHAPES[3]),
        )
    )
    spill = extra[:16].reshape(SPILL, 8 * STREAM)
    mixed = jnp.concatenate([mixed, spill[:, :WIDE]], axis=0)
    exact = lax.Precision.HIGHEST
    return (
        output_tokens,
        grad_tokens,
        mixed[:, :D].reshape(-1),
        mixed[:, D : D + KV].reshape(-1),
        mixed[:, D + KV : D + 2 * KV].reshape(-1),
        dot(mixed[:, D + 2 * KV :], columns.astype(jnp.float32), (1, 1), exact).reshape(-1),
        jnp.concatenate([gate_part, spill[:, WIDE : 2 * WIDE]], axis=0).reshape(-1),
        jnp.concatenate([up_part, spill[:, 2 * WIDE : 3 * WIDE]], axis=0).reshape(-1),
        dot(extra[16:], stream.astype(jnp.float32), (1, 1), exact).reshape(-1),
        extra[7, 128 : 128 + share],
    )


def solution(mesh):
    placed = (
        P("fsdp", None),
        P("fsdp"),
        P("fsdp"),
        P("fsdp"),
        P("fsdp"),
        P("fsdp"),
        P("fsdp"),
        P("fsdp"),
        P("fsdp"),
        P("fsdp"),
        P("fsdp", None),
    )
    return jax.shard_map(
        packed_device if mesh.shape["fsdp"] == DEVICES else per_device,
        mesh=mesh,
        in_specs=placed,
        out_specs=(
            P("fsdp", None),
            P("fsdp", None),
            P("fsdp"),
            P("fsdp"),
            P("fsdp"),
            P("fsdp"),
            P("fsdp"),
            P("fsdp"),
            P("fsdp"),
            P("fsdp"),
        ),
        check_vma=False,
    )
```

```python
import jax
import jax.numpy as jnp
import ml_dtypes
import numpy as np
from jax import lax
from jax.experimental import pallas as pl
from jax.experimental.pallas import tpu as pltpu
from jax.sharding import PartitionSpec as P

HEADS = 9
KV_HEADS = 3
HEAD_DIM = 64
FF = 1536
D = 576
KV = 192


ROPE_BASE = 100000.0
NORM_EPSILON = 1e-05
NEG_LARGE = -1e30


def unpack(flat_arrays):
    return (
        flat_arrays[0].reshape(D, D),
        flat_arrays[1].reshape(D, KV),
        flat_arrays[2].reshape(D, KV),
        flat_arrays[3].reshape(D, D),
        flat_arrays[4].reshape(D, FF),
        flat_arrays[5].reshape(D, FF),
        flat_arrays[6].reshape(FF, D),
        flat_arrays[7][:D].astype(jnp.float32),
        flat_arrays[7][D : 2 * D].astype(jnp.float32),
    )


def normalize_parts(values):
    inverse_root = lax.rsqrt(jnp.mean(values * values, axis=-1, keepdims=True) + NORM_EPSILON)
    return (values * inverse_root, inverse_root)


def norm_backward(grad_in, normed, inverse_root, gain_row):
    scaled = grad_in * gain_row
    return inverse_root * (scaled - normed * jnp.mean(scaled * normed, axis=-1, keepdims=True))


def rotate(values, cosine, sine_table):
    half_dim = values.shape[-1] // 2
    first_half = values[..., :half_dim]
    second_half = values[..., half_dim:]
    return jnp.concatenate(
        [
            first_half * cosine - second_half * sine_table,
            second_half * cosine + first_half * sine_table,
        ],
        axis=-1,
    )


def rotate_back(values, cosine, sine_table):
    half_dim = values.shape[-1] // 2
    first_half = values[..., :half_dim]
    second_half = values[..., half_dim:]
    return jnp.concatenate(
        [
            first_half * cosine + second_half * sine_table,
            second_half * cosine - first_half * sine_table,
        ],
        axis=-1,
    )


def per_device(
    tokens, segments, w_query, w_key, w_value, w_output, w_gate, w_up, w_down, gains, cotangent
):
    token_count = tokens.shape[0]
    group_size = HEADS // KV_HEADS
    score_scale = HEAD_DIM ** (-0.5)
    gain_length = gains.shape[0] * lax.axis_size("fsdp")
    gathered = (
        lax.all_gather(w_query, "fsdp", axis=0, tiled=True),
        lax.all_gather(w_key, "fsdp", axis=0, tiled=True),
        lax.all_gather(w_value, "fsdp", axis=0, tiled=True),
        lax.all_gather(w_output, "fsdp", axis=0, tiled=True),
        lax.all_gather(w_gate, "fsdp", axis=0, tiled=True),
        lax.all_gather(w_up, "fsdp", axis=0, tiled=True),
        lax.all_gather(w_down, "fsdp", axis=0, tiled=True),
        lax.all_gather(gains, "fsdp", axis=0, tiled=True),
    )
    (
        query_matrix,
        key_matrix,
        value_matrix,
        output_matrix,
        gate_matrix,
        up_matrix,
        down_matrix,
        gain_first,
        gain_second,
    ) = unpack(gathered)
    column = jnp.arange(token_count)[None, :]
    row_index = jnp.arange(token_count)[:, None]
    same_segment = segments[:, None] == segments[None, :]
    positions = jnp.sum((same_segment & (column < row_index)).astype(jnp.int32), axis=1)
    allowed = same_segment & (column <= row_index)
    frequency = ROPE_BASE ** (-(2.0 * jnp.arange(HEAD_DIM // 2).astype(jnp.float32)) / HEAD_DIM)
    angles = positions.astype(jnp.float32)[:, None] * frequency[None, :]
    cosine = jnp.cos(angles)[:, None, :]
    sine_table = jnp.sin(angles)[:, None, :]
    live_rows = (segments >= 0).astype(jnp.float32)[:, None]
    token_values = tokens.astype(jnp.float32)
    normed_one, root_one = normalize_parts(token_values)
    input_one = (normed_one * gain_first).astype(jnp.bfloat16)
    query_pre = jnp.dot(input_one, query_matrix, preferred_element_type=jnp.float32)
    key_pre = jnp.dot(input_one, key_matrix, preferred_element_type=jnp.float32)
    value_low = jnp.dot(input_one, value_matrix, preferred_element_type=jnp.float32).astype(
        jnp.bfloat16
    )
    value_low = value_low.reshape(token_count, KV_HEADS, HEAD_DIM)
    query_low = rotate(query_pre.reshape(token_count, HEADS, HEAD_DIM), cosine, sine_table).astype(
        jnp.bfloat16
    )
    query_low = query_low.reshape(token_count, KV_HEADS, group_size, HEAD_DIM)
    key_low = rotate(key_pre.reshape(token_count, KV_HEADS, HEAD_DIM), cosine, sine_table).astype(
        jnp.bfloat16
    )
    block_rows = min(token_count, 512)
    block_count = token_count // block_rows

    def masked_scores():
        scores = (
            jnp.einsum("qkgd,tkd->kgqt", query_low, key_low, preferred_element_type=jnp.float32)
            * score_scale
        )
        return (query_low, jnp.where(allowed, scores, NEG_LARGE))

    def attend(block_index):
        query_block, scores = masked_scores()
        row_peak = jnp.max(scores, axis=-1, keepdims=True)
        exponentials = jnp.exp(scores - row_peak)
        totals = jnp.sum(exponentials, axis=-1, keepdims=True)
        probabilities = (exponentials / totals).astype(jnp.bfloat16)
        attended = jnp.einsum(
            "kgqt,tkd->qkgd", probabilities, value_low, preferred_element_type=jnp.float32
        )
        return (attended.astype(jnp.bfloat16), row_peak[..., 0] + jnp.log(totals[..., 0]))

    attended_blocks, log_totals = lax.map(attend, jnp.arange(block_count))
    attended_low = attended_blocks.reshape(token_count, D)
    branch = jnp.dot(attended_low, output_matrix, preferred_element_type=jnp.float32)
    middle = token_values + branch
    normed_two, root_two = normalize_parts(middle)
    input_two = (normed_two * gain_second).astype(jnp.bfloat16)
    gate_pre = jnp.dot(input_two, gate_matrix, preferred_element_type=jnp.float32)
    up_pre = jnp.dot(input_two, up_matrix, preferred_element_type=jnp.float32)
    sigmoid_gate = jax.nn.sigmoid(gate_pre)
    silu_gate = gate_pre * sigmoid_gate
    product_low = (silu_gate * up_pre).astype(jnp.bfloat16)
    result = middle + jnp.dot(product_low, down_matrix, preferred_element_type=jnp.float32)
    output_tokens = (result * live_rows).astype(jnp.bfloat16)
    regathered = (
        lax.all_gather(w_query, "fsdp", axis=0, tiled=True),
        lax.all_gather(w_key, "fsdp", axis=0, tiled=True),
        lax.all_gather(w_value, "fsdp", axis=0, tiled=True),
        lax.all_gather(w_output, "fsdp", axis=0, tiled=True),
        lax.all_gather(w_gate, "fsdp", axis=0, tiled=True),
        lax.all_gather(w_up, "fsdp", axis=0, tiled=True),
        lax.all_gather(w_down, "fsdp", axis=0, tiled=True),
        lax.all_gather(gains, "fsdp", axis=0, tiled=True),
    )
    back_weights = unpack(regathered)
    (
        back_query,
        back_key,
        back_value,
        back_output,
        back_gate,
        back_up,
        back_down,
        back_first,
        back_second,
    ) = back_weights
    grad_result = cotangent.astype(jnp.float32) * live_rows
    grad_down_in = grad_result.astype(jnp.bfloat16)
    grad_down = jnp.einsum(
        "tf,td->fd", product_low, grad_down_in, preferred_element_type=jnp.float32
    )
    grad_product = jnp.einsum(
        "td,fd->tf", grad_down_in, back_down, preferred_element_type=jnp.float32
    )
    grad_gate_pre = (
        grad_product * up_pre * sigmoid_gate * (1.0 + gate_pre * (1.0 - sigmoid_gate))
    ).astype(jnp.bfloat16)
    grad_up_pre = (grad_product * silu_gate).astype(jnp.bfloat16)
    grad_gate = jnp.einsum(
        "td,tf->df", input_two, grad_gate_pre, preferred_element_type=jnp.float32
    )
    grad_up = jnp.einsum("td,tf->df", input_two, grad_up_pre, preferred_element_type=jnp.float32)
    grad_input_two = jnp.einsum(
        "tf,df->td", grad_gate_pre, back_gate, preferred_element_type=jnp.float32
    )
    grad_input_two = grad_input_two + jnp.einsum(
        "tf,df->td", grad_up_pre, back_up, preferred_element_type=jnp.float32
    )
    grad_gain_two = jnp.sum(grad_input_two * normed_two, axis=0)
    grad_middle = grad_result + norm_backward(grad_input_two, normed_two, root_two, back_second)
    grad_branch = grad_middle.astype(jnp.bfloat16)
    grad_output = jnp.einsum(
        "td,te->de", attended_low, grad_branch, preferred_element_type=jnp.float32
    )
    grad_attended = jnp.einsum(
        "te,de->td", grad_branch, back_output, preferred_element_type=jnp.float32
    ).astype(jnp.bfloat16)
    grad_attended = grad_attended.reshape(token_count, KV_HEADS, group_size, HEAD_DIM)

    def back_step(carried, inputs):
        grad_keys, grad_values = carried
        block_index, log_block = inputs
        query_block, scores = masked_scores()
        probabilities = jnp.exp(scores - log_block[..., None])
        grad_probs = jnp.einsum(
            "qkgd,tkd->kgqt", grad_attended, value_low, preferred_element_type=jnp.float32
        )
        centre = jnp.sum(probabilities * grad_probs, axis=-1, keepdims=True)
        grad_scores = (probabilities * (grad_probs - centre)).astype(jnp.bfloat16)
        grad_query_block = (
            jnp.einsum("kgqt,tkd->qkgd", grad_scores, key_low, preferred_element_type=jnp.float32)
            * score_scale
        )
        grad_keys = (
            grad_keys
            + jnp.einsum(
                "kgqt,qkgd->tkd", grad_scores, query_block, preferred_element_type=jnp.float32
            )
            * score_scale
        )
        grad_values = grad_values + jnp.einsum(
            "kgqt,qkgd->tkd",
            probabilities.astype(jnp.bfloat16),
            grad_attended,
            preferred_element_type=jnp.float32,
        )
        return ((grad_keys, grad_values), grad_query_block)

    zero_state = jnp.zeros((token_count, KV_HEADS, HEAD_DIM), jnp.float32)
    (grad_keys, grad_values), grad_query_blocks = lax.scan(
        back_step, (zero_state, zero_state), (jnp.arange(block_count), log_totals)
    )
    grad_query_low = rotate_back(
        grad_query_blocks.reshape(token_count, HEADS, HEAD_DIM), cosine, sine_table
    )
    grad_query_low = grad_query_low.astype(jnp.bfloat16).reshape(token_count, D)
    grad_key_low = (
        rotate_back(grad_keys, cosine, sine_table).astype(jnp.bfloat16).reshape(token_count, KV)
    )
    grad_value_low = grad_values.astype(jnp.bfloat16).reshape(token_count, KV)
    grad_query = jnp.einsum(
        "td,te->de", input_one, grad_query_low, preferred_element_type=jnp.float32
    )
    grad_key = jnp.einsum("td,te->de", input_one, grad_key_low, preferred_element_type=jnp.float32)
    grad_value = jnp.einsum(
        "td,te->de", input_one, grad_value_low, preferred_element_type=jnp.float32
    )
    grad_input_one = jnp.einsum(
        "te,de->td", grad_query_low, back_query, preferred_element_type=jnp.float32
    )
    grad_input_one = grad_input_one + jnp.einsum(
        "te,de->td", grad_key_low, back_key, preferred_element_type=jnp.float32
    )
    grad_input_one = grad_input_one + jnp.einsum(
        "te,de->td", grad_value_low, back_value, preferred_element_type=jnp.float32
    )
    grad_gain_one = jnp.sum(grad_input_one * normed_one, axis=0)
    grad_tokens = grad_middle + norm_backward(grad_input_one, normed_one, root_one, back_first)
    grad_gains = jnp.concatenate(
        [grad_gain_one, grad_gain_two, jnp.zeros((gain_length - 2 * D,), jnp.float32)]
    )
    shares = (
        lax.psum_scatter(grad_query.reshape(-1), "fsdp", scatter_dimension=0, tiled=True),
        lax.psum_scatter(grad_key.reshape(-1), "fsdp", scatter_dimension=0, tiled=True),
        lax.psum_scatter(grad_value.reshape(-1), "fsdp", scatter_dimension=0, tiled=True),
        lax.psum_scatter(grad_output.reshape(-1), "fsdp", scatter_dimension=0, tiled=True),
        lax.psum_scatter(grad_gate.reshape(-1), "fsdp", scatter_dimension=0, tiled=True),
        lax.psum_scatter(grad_up.reshape(-1), "fsdp", scatter_dimension=0, tiled=True),
        lax.psum_scatter(grad_down.reshape(-1), "fsdp", scatter_dimension=0, tiled=True),
        lax.psum_scatter(grad_gains, "fsdp", scatter_dimension=0, tiled=True),
    )
    return (
        output_tokens,
        grad_tokens.astype(jnp.bfloat16),
        shares[0],
        shares[1],
        shares[2],
        shares[3],
        shares[4],
        shares[5],
        shares[6],
        shares[7],
    )


AXIS_SIZES = (4, 2, 2, 2)
ARRAYS = 4
WIDE = 1536
NARROW = 640
SHAPES = ((16, WIDE), (16, WIDE), (16, WIDE), (64, NARROW))
MESH = pl.DeviceIdType.MESH
PIECES = (
    (0, 0, 16, 0, 768, (1, 0, 2)),
    (0, 0, 16, 768, 768, (2, 0, 1)),
    (1, 0, 16, 0, 768, (1, 0, 2)),
    (1, 0, 16, 768, 768, (2, 0, 1)),
    (2, 0, 16, 0, 768, (0, 1, 2)),
    (2, 0, 16, 768, 768, (0, 2, 1)),
    (3, 0, 32, 0, NARROW, (0, 1, 2)),
    (3, 32, 32, 0, NARROW, (0, 2, 1)),
)


def window(piece):
    return (pl.ds(piece[1], piece[2]), pl.ds(piece[3], piece[4]))


def coordinates():
    me = lax.axis_index("fsdp")
    return [me // 8, (me // 4) % 2, (me // 2) % 2, me % 2]


def device_at(coords):
    return ((coords[0] * 2 + coords[1]) * 2 + coords[2]) * 2 + coords[3]


def peers_along(coords, dim):
    found = []
    for offset in range(1, AXIS_SIZES[dim]):
        other = list(coords)
        other[dim] = lax.rem(coords[dim] + offset, AXIS_SIZES[dim])
        found.append(other)
    return found


def enter(coords):
    barrier = pltpu.get_barrier_semaphore()
    count = 0
    for dim in range(4):
        for other in peers_along(coords, dim):
            pl.semaphore_signal(barrier, inc=1, device_id=(device_at(other),), device_id_type=MESH)
            count += 1
    pl.semaphore_wait(barrier, count)


def gather_kernel(*refs):
    ins, outs = refs[:ARRAYS], refs[ARRAYS : 2 * ARRAYS]
    send_sem, recv_sem = refs[2 * ARRAYS :]
    coords = coordinates()
    enter(coords)

    for which in range(ARRAYS):
        outs[which][coords[0], coords[1], coords[2], coords[3]] = ins[which][...]

    def run(which, piece):
        out = outs[piece[0]]
        counter = [0]
        index = list(coords)
        sibling = peers_along(coords, 3)[0]
        core_copies = []

        def push(block, target):
            slot = counter[0]
            counter[0] += 1
            view = out.at[tuple(block) + window(piece)]
            copy = pltpu.make_async_remote_copy(
                src_ref=view,
                dst_ref=view,
                send_sem=send_sem.at[which, slot],
                recv_sem=recv_sem.at[which, slot],
                device_id=(device_at(target),),
                device_id_type=MESH,
            )
            copy.start()
            return copy

        pending_core = [list(index)]
        for dim in piece[5]:
            copies = [push(index, other) for other in peers_along(coords, dim)]
            for block in pending_core:
                core_copies.append(push(block, sibling))
            pending_core = []
            yield
            for offset, copy in enumerate(copies):
                copy.wait()
                block = list(index)
                size = AXIS_SIZES[dim]
                block[dim] = lax.rem(coords[dim] + size - offset - 1, size)
                pending_core.append(block)
            index[dim] = slice(None)
        for block in pending_core:
            core_copies.append(push(block, sibling))
        yield
        for copy in core_copies:
            copy.wait()

    drive([run(which, piece) for which, piece in enumerate(PIECES)])


def drive(tasks):
    while tasks:
        kept = []
        for task in tasks:
            try:
                next(task)
                kept.append(task)
            except StopIteration:
                pass
        tasks = kept


def scatter_kernel(*refs):
    ins, outs = refs[:ARRAYS], refs[ARRAYS : 2 * ARRAYS]
    landing = refs[2 * ARRAYS : -2]
    send_sem, recv_sem = refs[-2:]
    coords = coordinates()
    enter(coords)

    def run(which, piece):
        order = (3,) + tuple(reversed(piece[5]))
        remaining = [0, 1, 2, 3]
        current = ins[piece[0]]
        counter = [0]

        def push(stage, dim, part, offset, target):
            slot = counter[0]
            counter[0] += 1
            index = tuple(
                part if axis == dim else slice(None) for axis in remaining
            )
            if stage == 0:
                index = index + window(piece)
            land = landing[which * 4 + stage]
            copy = pltpu.make_async_remote_copy(
                src_ref=current.at[index],
                dst_ref=land.at[offset],
                send_sem=send_sem.at[which, slot],
                recv_sem=recv_sem.at[which, slot],
                device_id=(device_at(target),),
                device_id_type=MESH,
            )
            copy.start()
            return copy

        copies = [
            push(0, 3, other[3], offset, other)
            for offset, other in enumerate(peers_along(coords, 3))
        ]
        for stage, dim in enumerate(order):
            yield
            for copy in copies:
                copy.wait()
            land = landing[which * 4 + stage]
            rest = [axis for axis in remaining if axis != dim]
            last = stage == 3

            def add_group(fixed, current=current, land=land, rest=rest, dim=dim, last=last, held=tuple(remaining), first=stage == 0):
                loose = [axis for axis in rest if axis not in fixed]
                total = 1
                for axis in loose:
                    total *= AXIS_SIZES[axis]

                def body(step, carry):
                    at = dict(fixed)
                    left = step
                    for axis in reversed(loose):
                        at[axis] = left % AXIS_SIZES[axis]
                        left = left // AXIS_SIZES[axis]
                    mine = tuple(coords[dim] if axis == dim else at[axis] for axis in held)
                    target = tuple(at[axis] for axis in rest)
                    if first:
                        mine = mine + window(piece)
                    value = current[mine].astype(jnp.float32)
                    for offset in range(AXIS_SIZES[dim] - 1):
                        value = value + land[(offset,) + target].astype(jnp.float32)
                    if last:
                        outs[piece[0]][window(piece)] = value
                    else:
                        land[(0,) + target] = value.astype(jnp.bfloat16)
                    return carry

                if total == 1:
                    body(0, 0)
                else:
                    lax.fori_loop(0, total, body, 0)

            if last:
                add_group({})
                break
            following = order[stage + 1]
            remaining = rest
            current = land.at[0]
            copies = []
            for offset, other in enumerate(peers_along(coords, following)):
                add_group({following: other[following]})
                copies.append(push(stage + 1, following, other[following], offset, other))
            add_group({following: coords[following]})

    drive([run(which, piece) for which, piece in enumerate(PIECES)])


def gather_packed(parts):
    return pl.pallas_call(
        gather_kernel,
        out_shape=tuple(jax.ShapeDtypeStruct(AXIS_SIZES + shape, jnp.bfloat16) for shape in SHAPES),
        in_specs=[pl.BlockSpec(memory_space=pltpu.VMEM)] * ARRAYS,
        out_specs=tuple([pl.BlockSpec(memory_space=pltpu.VMEM)] * ARRAYS),
        scratch_shapes=[
            pltpu.SemaphoreType.DMA((len(PIECES), 12)),
            pltpu.SemaphoreType.DMA((len(PIECES), 12)),
        ],
        compiler_params=pltpu.CompilerParams(
            collective_id=0, has_side_effects=True, vmem_limit_bytes=32 * 1024 * 1024
        ),
        name="gather_weights",
    )(*parts)


def scatter_packed(parts):
    landing = []
    for piece in PIECES:
        remaining = [0, 1, 2, 3]
        for dim in (3,) + tuple(reversed(piece[5])):
            remaining = [axis for axis in remaining if axis != dim]
            extent = tuple(AXIS_SIZES[axis] for axis in remaining)
            landing.append(
                pltpu.VMEM((AXIS_SIZES[dim] - 1,) + extent + (piece[2], piece[4]), jnp.bfloat16)
            )
    return pl.pallas_call(
        scatter_kernel,
        out_shape=tuple(jax.ShapeDtypeStruct(shape, jnp.float32) for shape in SHAPES),
        in_specs=[pl.BlockSpec(memory_space=pltpu.VMEM)] * ARRAYS,
        out_specs=tuple([pl.BlockSpec(memory_space=pltpu.VMEM)] * ARRAYS),
        scratch_shapes=landing
        + [
            pltpu.SemaphoreType.DMA((len(PIECES), 8)),
            pltpu.SemaphoreType.DMA((len(PIECES), 8)),
        ],
        compiler_params=pltpu.CompilerParams(
            collective_id=1, has_side_effects=True, vmem_limit_bytes=40 * 1024 * 1024
        ),
        name="scatter_gradients",
    )(*parts)


DEVICES = 32
ROWS = D // DEVICES
DOWN_ROWS = FF // DEVICES
SPILL = ROWS - 16


STREAM = 640
CHUNK = 512
PER_GAIN = 36


def order_matrices():
    main = (np.arange(DEVICES)[:, None] * ROWS + np.arange(16)[None, :]).reshape(-1)
    spill = (np.arange(DEVICES)[:, None] * ROWS + 16 + np.arange(SPILL)[None, :]).reshape(-1)
    stream = np.zeros((D, STREAM), np.float32)
    stream[main, np.arange(512)] = 1.0
    stream[spill, 576 + np.arange(64)] = 1.0
    columns = np.concatenate([stream[:, 576:], stream[:, :512]], axis=1)
    select = np.zeros((512, 512), np.float32)
    for part in range(8):
        for owner in range(DEVICES):
            for row in range(SPILL):
                select[part * 64 + owner * 2 + row, owner * 16 + row * 8 + part] = 1.0
    true_index = np.full((STREAM,), -1)
    true_index[:512] = main
    true_index[576:] = spill
    pick = np.zeros((2, 64, STREAM), np.float32)
    holder = np.zeros((2, 64, STREAM), np.float32)
    for half in range(2):
        for lane in range(STREAM):
            if true_index[lane] >= 0:
                flat = half * D + true_index[lane]
                pick[half, flat % PER_GAIN, lane] = 1.0
                holder[half, 2 * (flat // PER_GAIN), lane] = 1.0
    return tuple(value.astype(ml_dtypes.bfloat16) for value in (stream, columns, select, pick, holder))


def dot(left, right, contract=(1, 0), precision=None):
    return lax.dot_general(
        left,
        right,
        (((contract[0],), (contract[1],)), ((), ())),
        preferred_element_type=jnp.float32,
        precision=precision,
    )


def low_dot(left, right, contract=(1, 0)):
    return dot(left, right, contract).astype(jnp.bfloat16)


def swap_halves(values):
    width = values.shape[1]
    lane = lax.broadcasted_iota(jnp.int32, values.shape, 1)
    return jnp.where(
        lane % HEAD_DIM < HEAD_DIM // 2,
        pltpu.roll(values, width - HEAD_DIM // 2, 1),
        pltpu.roll(values, HEAD_DIM // 2, 1),
    )


def stream_norm(values):
    root = lax.rsqrt(jnp.sum(values * values, axis=1, keepdims=True) * (1.0 / D) + NORM_EPSILON)
    return values * root, root


def stream_norm_back(grad_in, normed, root, gain_row):
    scaled = grad_in * gain_row
    mean = jnp.sum(scaled * normed, axis=1, keepdims=True) * (1.0 / D)
    return root * (scaled - normed * mean)


def layer_kernel(
    tokens, cotangent, seg_row, seg_col, cosine, sine, stream, select, pick, holder,
    mixed, gate, up, extra,
    out_tokens, out_grad_tokens, g_mixed, g_gate, g_up, g_extra,
    w_spill, w_down, g_spill, probs, heads, attended, g_heads, result, g_input,
):
    low = jnp.bfloat16
    count = tokens.shape[0]
    scale = HEAD_DIM ** (-0.5)
    spill_in = extra[:, :16, :].reshape(512, STREAM)
    spill_rows = low_dot(select[...], spill_in)
    w_spill[0:64, :] = jnp.zeros((64, 8 * STREAM), low)
    for part in range(8):
        w_spill[64:128, part * STREAM : (part + 1) * STREAM] = spill_rows[part * 64 : part * 64 + 64]
    w_down[...] = extra[:, 16:, :].reshape(FF, STREAM)
    gain_block = spill_rows[448:512, 128:192]
    gains = [
        jnp.sum(dot(gain_block, pick[half]) * holder[half].astype(jnp.float32), axis=0, keepdims=True)
        for half in range(2)
    ]

    values = dot(tokens[...], stream[...])
    live = (seg_col[...] >= 0).astype(jnp.float32)
    grad_result = dot(cotangent[...], stream[...]) * live
    grad_down_in = grad_result.astype(low)
    normed_one, root_one = stream_norm(values)
    input_one = (normed_one * gains[0]).astype(low)
    one_main, one_spill = input_one[:, :512], input_one[:, 512:]
    qkv = dot(one_main, mixed[:, :1024]) + dot(one_spill, w_spill[:, :1024])
    wide_cos = jnp.concatenate([cosine[...]] * 6, axis=1)
    wide_sin = jnp.concatenate([sine[...]] * 6, axis=1)
    turning = qkv[:, :768]
    heads[:, :768] = (turning * wide_cos + swap_halves(turning) * wide_sin).astype(low)
    heads[:, 768:] = qkv[:, 768:].astype(low)
    column = lax.broadcasted_iota(jnp.int32, (count, count), 1)
    row = lax.broadcasted_iota(jnp.int32, (count, count), 0)
    allowed = (seg_col[...] == seg_row[...]) & (column <= row)

    def head(array, start):
        return array[:, start : start + HEAD_DIM]

    for h in range(HEADS):
        c = h // 3
        scores = dot(head(heads, 64 * h), head(heads, 576 + 64 * c), (1, 1)) * scale
        scores = jnp.where(allowed, scores, NEG_LARGE)
        peak = jnp.max(scores, axis=1, keepdims=True)
        powers = jnp.exp(scores - peak)
        p = powers / jnp.sum(powers, axis=1, keepdims=True)
        probs[h] = p
        attended[:, 64 * h : 64 * h + 64] = low_dot(p.astype(low), head(heads, 768 + 64 * c))
    att = low_dot(attended[...], stream[...])
    att_main, att_spill = att[:, :512], att[:, 512:]
    branch_main = dot(att_main, mixed[:, 1024:]) + dot(att_spill, w_spill[:, 1024:1536])
    branch_spill = dot(att_main, mixed[:, 896:1024]) + dot(att_spill, w_spill[:, 896:1024])
    lane = lax.broadcasted_iota(jnp.int32, branch_spill.shape, 1)
    branch_spill = jnp.where(lane >= 64, branch_spill, 0.0)
    middle = values + jnp.concatenate([branch_main, branch_spill], axis=1)
    normed_two, root_two = stream_norm(middle)
    input_two = (normed_two * gains[1]).astype(low)
    two_main, two_spill = input_two[:, :512], input_two[:, 512:]
    result[...] = middle
    g_input[...] = jnp.zeros_like(g_input)

    for start in range(0, FF, CHUNK):
        here = slice(start, start + CHUNK)
        gate_at = slice(FF + start, FF + start + CHUNK)
        up_at = slice(2 * FF + start, 2 * FF + start + CHUNK)
        gate_pre = dot(two_main, gate[:, here]) + dot(two_spill, w_spill[:, gate_at])
        up_pre = dot(two_main, up[:, here]) + dot(two_spill, w_spill[:, up_at])
        sig = 1.0 / (1.0 + jnp.exp(-gate_pre))
        silu = gate_pre * sig
        product = (silu * up_pre).astype(low)
        down = w_down[here, :]
        result[...] += dot(product, down)
        w_down_grad = low_dot(product, grad_down_in, (0, 0))
        g_product = dot(grad_down_in, down, (1, 1))
        gg = (g_product * up_pre * sig * (1.0 + gate_pre * (1.0 - sig))).astype(low)
        gu = (g_product * silu).astype(low)
        g_input[:, :512] += dot(gg, gate[:, here], (1, 1)) + dot(gu, up[:, here], (1, 1))
        g_input[:, 512:] += dot(gg, w_spill[:, gate_at], (1, 1)) + dot(gu, w_spill[:, up_at], (1, 1))
        g_gate[:, here] = low_dot(two_main, gg, (0, 0))
        g_up[:, here] = low_dot(two_main, gu, (0, 0))
        g_spill[:, gate_at] = low_dot(two_spill, gg, (0, 0))[64:]
        g_spill[:, up_at] = low_dot(two_spill, gu, (0, 0))[64:]
        w_down[here, :] = w_down_grad
    g_extra[:, 16:, :] = w_down[...].reshape(DEVICES, DOWN_ROWS, STREAM)
    out_tokens[...] = low_dot((result[...] * live).astype(low), stream[...], (1, 1))

    grad_input_two = g_input[...]
    gain_grads = [None, jnp.sum(grad_input_two * normed_two, axis=0, keepdims=True)]
    grad_middle = grad_result + stream_norm_back(grad_input_two, normed_two, root_two, gains[1])
    grad_branch = grad_middle.astype(low)
    branch_main, branch_spill = grad_branch[:, :512], grad_branch[:, 512:]
    g_mixed[:, 1024:] = low_dot(att_main, branch_main, (0, 0))
    g_spill[:, 1024:1536] = low_dot(att_spill, branch_main, (0, 0))[64:]
    g_att = jnp.concatenate(
        [
            dot(branch_main, mixed[:, 1024:], (1, 1)) + dot(branch_spill, mixed[:, 896:1024], (1, 1)),
            dot(branch_main, w_spill[:, 1024:1536], (1, 1))
            + dot(branch_spill, w_spill[:, 896:1024], (1, 1)),
        ],
        axis=1,
    )
    attended[...] = low_dot(g_att.astype(low), stream[...], (1, 1))
    g_heads[:, 896:] = jnp.zeros((count, 128), jnp.float32)
    for c in range(KV_HEADS):
        keys, vals = head(heads, 576 + 64 * c), head(heads, 768 + 64 * c)
        g_keys, g_vals = 0.0, 0.0
        for h in range(3 * c, 3 * c + 3):
            p, g_a, q = probs[h], head(attended, 64 * h), head(heads, 64 * h)
            gp = dot(g_a, vals, (1, 1))
            centre = jnp.sum(p * gp, axis=1, keepdims=True)
            gs = (p * (gp - centre)).astype(low)
            g_heads[:, 64 * h : 64 * h + 64] = dot(gs, keys) * scale
            g_keys = g_keys + dot(gs, q, (0, 0))
            g_vals = g_vals + dot(p.astype(low), g_a, (0, 0))
        g_heads[:, 576 + 64 * c : 640 + 64 * c] = g_keys * scale
        g_heads[:, 768 + 64 * c : 832 + 64 * c] = g_vals
    turning = g_heads[:, :768]
    grad_qkv = jnp.concatenate(
        [turning * wide_cos - swap_halves(turning) * wide_sin, g_heads[:, 768:]], axis=1
    ).astype(low)
    g_mixed[:, :896] = low_dot(one_main, grad_qkv[:, :896], (0, 0))
    g_spill[:, :896] = low_dot(one_spill, grad_qkv[:, :896], (0, 0))[64:]
    tail = grad_qkv[:, 896:]
    g_mixed[:, 896:1024] = (dot(one_main, tail, (0, 0)) + dot(att_main, branch_spill, (0, 0))).astype(low)
    g_spill[:, 896:1024] = (dot(one_spill, tail, (0, 0)) + dot(att_spill, branch_spill, (0, 0))).astype(low)[64:]
    grad_input_one = jnp.concatenate(
        [dot(grad_qkv, mixed[:, :1024], (1, 1)), dot(grad_qkv, w_spill[:, :1024], (1, 1))], axis=1
    )
    gain_grads[0] = jnp.sum(grad_input_one * normed_one, axis=0, keepdims=True)
    grad_tokens = grad_middle + stream_norm_back(grad_input_one, normed_one, root_one, gains[0])
    out_grad_tokens[...] = low_dot(grad_tokens.astype(low), stream[...], (1, 1))
    block = 0.0
    for half in range(2):
        spread = holder[half].astype(jnp.float32) * gain_grads[half]
        block = block + dot(spread.astype(low), pick[half], (1, 1))
    g_spill[:, 3 * FF :] = jnp.concatenate(
        [block, jnp.zeros((64, 8 * STREAM - 3 * FF - 64), jnp.float32)], axis=1
    ).astype(low)
    stacked = jnp.concatenate(
        [g_spill[:, part * STREAM : (part + 1) * STREAM] for part in range(8)], axis=0
    )
    g_extra[:, :16, :] = low_dot(select[...], stacked, (0, 0)).reshape(DEVICES, 16, STREAM)


def local_layer(*operands):
    count = operands[0].shape[0]
    low = jnp.bfloat16
    vmem = pl.BlockSpec(memory_space=pltpu.VMEM)
    return pl.pallas_call(
        layer_kernel,
        out_shape=(
            jax.ShapeDtypeStruct((count, D), low),
            jax.ShapeDtypeStruct((count, D), low),
            jax.ShapeDtypeStruct((512, WIDE), low),
            jax.ShapeDtypeStruct((512, WIDE), low),
            jax.ShapeDtypeStruct((512, WIDE), low),
            jax.ShapeDtypeStruct((DEVICES, 64, STREAM), low),
        ),
        in_specs=[vmem] * len(operands),
        out_specs=(vmem,) * 6,
        scratch_shapes=[
            pltpu.VMEM((128, 8 * STREAM), low),
            pltpu.VMEM((FF, STREAM), low),
            pltpu.VMEM((64, 8 * STREAM), low),
            pltpu.VMEM((HEADS, count, count), jnp.float32),
            pltpu.VMEM((count, 1024), low),
            pltpu.VMEM((count, D), low),
            pltpu.VMEM((count, 1024), jnp.float32),
            pltpu.VMEM((count, STREAM), jnp.float32),
            pltpu.VMEM((count, STREAM), jnp.float32),
        ],
        compiler_params=pltpu.CompilerParams(vmem_limit_bytes=52 * 1024 * 1024),
        name="local_layer",
    )(*operands)


def packed_device(
    tokens, segments, w_query, w_key, w_value, w_output, w_gate, w_up, w_down, gains, cotangent
):
    token_count = tokens.shape[0]
    stream, columns, select, pick, holder = (jnp.asarray(value) for value in order_matrices())
    share = gains.shape[0]
    rows = jnp.concatenate(
        [
            w_query.reshape(ROWS, D),
            w_key.reshape(ROWS, KV),
            w_value.reshape(ROWS, KV),
            low_dot(w_output.reshape(ROWS, D), columns),
            w_gate.reshape(ROWS, FF),
            w_up.reshape(ROWS, FF),
        ],
        axis=1,
    )
    down_rows = low_dot(w_down.reshape(DOWN_ROWS, D), stream)
    spare = jnp.pad(gains.reshape(1, share), ((0, 1), (0, 8 * STREAM - 3 * FF - share)))
    spill = jnp.concatenate([rows[16:], spare], axis=1).reshape(16, STREAM)
    weights = gather_packed(
        (
            rows[:16, :WIDE],
            rows[:16, WIDE : 2 * WIDE],
            rows[:16, 2 * WIDE :],
            jnp.concatenate([spill, down_rows], axis=0),
        )
    )
    column = jnp.arange(token_count)[None, :]
    row_index = jnp.arange(token_count)[:, None]
    same_segment = segments[:, None] == segments[None, :]
    positions = jnp.sum((same_segment & (column < row_index)).astype(jnp.int32), axis=1)
    frequency = ROPE_BASE ** (-(2.0 * jnp.arange(HEAD_DIM // 2).astype(jnp.float32)) / HEAD_DIM)
    angles = positions.astype(jnp.float32)[:, None] * frequency[None, :]
    cosine, sine = jnp.cos(angles), jnp.sin(angles)
    output_tokens, grad_tokens, g_mixed, g_gate, g_up, g_extra = local_layer(
        tokens,
        cotangent,
        segments[None, :],
        segments[:, None],
        jnp.concatenate([cosine] * 4, axis=1),
        jnp.concatenate([-sine, sine, -sine, sine], axis=1),
        stream,
        select,
        pick,
        holder,
        weights[0].reshape(512, WIDE),
        weights[1].reshape(512, WIDE),
        weights[2].reshape(512, WIDE),
        weights[3].reshape(DEVICES, 64, STREAM),
    )
    mixed, gate_part, up_part, extra = scatter_packed(
        (
            g_mixed.reshape(AXIS_SIZES + SHAPES[0]),
            g_gate.reshape(AXIS_SIZES + SHAPES[1]),
            g_up.reshape(AXIS_SIZES + SHAPES[2]),
            g_extra.reshape(AXIS_SIZES + SHAPES[3]),
        )
    )
    spill = extra[:16].reshape(SPILL, 8 * STREAM)
    mixed = jnp.concatenate([mixed, spill[:, :WIDE]], axis=0)
    exact = lax.Precision.HIGHEST
    return (
        output_tokens,
        grad_tokens,
        mixed[:, :D].reshape(-1),
        mixed[:, D : D + KV].reshape(-1),
        mixed[:, D + KV : D + 2 * KV].reshape(-1),
        dot(mixed[:, D + 2 * KV :], columns.astype(jnp.float32), (1, 1), exact).reshape(-1),
        jnp.concatenate([gate_part, spill[:, WIDE : 2 * WIDE]], axis=0).reshape(-1),
        jnp.concatenate([up_part, spill[:, 2 * WIDE : 3 * WIDE]], axis=0).reshape(-1),
        dot(extra[16:], stream.astype(jnp.float32), (1, 1), exact).reshape(-1),
        extra[7, 128 : 128 + share],
    )


def solution(mesh):
    placed = (
        P("fsdp", None),
        P("fsdp"),
        P("fsdp"),
        P("fsdp"),
        P("fsdp"),
        P("fsdp"),
        P("fsdp"),
        P("fsdp"),
        P("fsdp"),
        P("fsdp"),
        P("fsdp", None),
    )
    return jax.shard_map(
        packed_device if mesh.shape["fsdp"] == DEVICES else per_device,
        mesh=mesh,
        in_specs=placed,
        out_specs=(
            P("fsdp", None),
            P("fsdp", None),
            P("fsdp"),
            P("fsdp"),
            P("fsdp"),
            P("fsdp"),
            P("fsdp"),
            P("fsdp"),
            P("fsdp"),
            P("fsdp"),
        ),
        check_vma=False,
    )
```

```python
import jax
import jax.numpy as jnp
import ml_dtypes
import numpy as np
from jax import lax
from jax.experimental import pallas as pl
from jax.experimental.pallas import tpu as pltpu
from jax.sharding import PartitionSpec as P

HEADS = 9
KV_HEADS = 3
HEAD_DIM = 64
FF = 1536
D = 576
KV = 192


ROPE_BASE = 100000.0
NORM_EPSILON = 1e-05
NEG_LARGE = -1e30


def unpack(flat_arrays):
    return (
        flat_arrays[0].reshape(D, D),
        flat_arrays[1].reshape(D, KV),
        flat_arrays[2].reshape(D, KV),
        flat_arrays[3].reshape(D, D),
        flat_arrays[4].reshape(D, FF),
        flat_arrays[5].reshape(D, FF),
        flat_arrays[6].reshape(FF, D),
        flat_arrays[7][:D].astype(jnp.float32),
        flat_arrays[7][D : 2 * D].astype(jnp.float32),
    )


def normalize_parts(values):
    inverse_root = lax.rsqrt(jnp.mean(values * values, axis=-1, keepdims=True) + NORM_EPSILON)
    return (values * inverse_root, inverse_root)


def norm_backward(grad_in, normed, inverse_root, gain_row):
    scaled = grad_in * gain_row
    return inverse_root * (scaled - normed * jnp.mean(scaled * normed, axis=-1, keepdims=True))


def rotate(values, cosine, sine_table):
    half_dim = values.shape[-1] // 2
    first_half = values[..., :half_dim]
    second_half = values[..., half_dim:]
    return jnp.concatenate(
        [
            first_half * cosine - second_half * sine_table,
            second_half * cosine + first_half * sine_table,
        ],
        axis=-1,
    )


def rotate_back(values, cosine, sine_table):
    half_dim = values.shape[-1] // 2
    first_half = values[..., :half_dim]
    second_half = values[..., half_dim:]
    return jnp.concatenate(
        [
            first_half * cosine + second_half * sine_table,
            second_half * cosine - first_half * sine_table,
        ],
        axis=-1,
    )


def per_device(
    tokens, segments, w_query, w_key, w_value, w_output, w_gate, w_up, w_down, gains, cotangent
):
    token_count = tokens.shape[0]
    group_size = HEADS // KV_HEADS
    score_scale = HEAD_DIM ** (-0.5)
    gain_length = gains.shape[0] * lax.axis_size("fsdp")
    gathered = (
        lax.all_gather(w_query, "fsdp", axis=0, tiled=True),
        lax.all_gather(w_key, "fsdp", axis=0, tiled=True),
        lax.all_gather(w_value, "fsdp", axis=0, tiled=True),
        lax.all_gather(w_output, "fsdp", axis=0, tiled=True),
        lax.all_gather(w_gate, "fsdp", axis=0, tiled=True),
        lax.all_gather(w_up, "fsdp", axis=0, tiled=True),
        lax.all_gather(w_down, "fsdp", axis=0, tiled=True),
        lax.all_gather(gains, "fsdp", axis=0, tiled=True),
    )
    (
        query_matrix,
        key_matrix,
        value_matrix,
        output_matrix,
        gate_matrix,
        up_matrix,
        down_matrix,
        gain_first,
        gain_second,
    ) = unpack(gathered)
    column = jnp.arange(token_count)[None, :]
    row_index = jnp.arange(token_count)[:, None]
    same_segment = segments[:, None] == segments[None, :]
    positions = jnp.sum((same_segment & (column < row_index)).astype(jnp.int32), axis=1)
    allowed = same_segment & (column <= row_index)
    frequency = ROPE_BASE ** (-(2.0 * jnp.arange(HEAD_DIM // 2).astype(jnp.float32)) / HEAD_DIM)
    angles = positions.astype(jnp.float32)[:, None] * frequency[None, :]
    cosine = jnp.cos(angles)[:, None, :]
    sine_table = jnp.sin(angles)[:, None, :]
    live_rows = (segments >= 0).astype(jnp.float32)[:, None]
    token_values = tokens.astype(jnp.float32)
    normed_one, root_one = normalize_parts(token_values)
    input_one = (normed_one * gain_first).astype(jnp.bfloat16)
    query_pre = jnp.dot(input_one, query_matrix, preferred_element_type=jnp.float32)
    key_pre = jnp.dot(input_one, key_matrix, preferred_element_type=jnp.float32)
    value_low = jnp.dot(input_one, value_matrix, preferred_element_type=jnp.float32).astype(
        jnp.bfloat16
    )
    value_low = value_low.reshape(token_count, KV_HEADS, HEAD_DIM)
    query_low = rotate(query_pre.reshape(token_count, HEADS, HEAD_DIM), cosine, sine_table).astype(
        jnp.bfloat16
    )
    query_low = query_low.reshape(token_count, KV_HEADS, group_size, HEAD_DIM)
    key_low = rotate(key_pre.reshape(token_count, KV_HEADS, HEAD_DIM), cosine, sine_table).astype(
        jnp.bfloat16
    )
    block_rows = min(token_count, 512)
    block_count = token_count // block_rows

    def masked_scores():
        scores = (
            jnp.einsum("qkgd,tkd->kgqt", query_low, key_low, preferred_element_type=jnp.float32)
            * score_scale
        )
        return (query_low, jnp.where(allowed, scores, NEG_LARGE))

    def attend(block_index):
        query_block, scores = masked_scores()
        row_peak = jnp.max(scores, axis=-1, keepdims=True)
        exponentials = jnp.exp(scores - row_peak)
        totals = jnp.sum(exponentials, axis=-1, keepdims=True)
        probabilities = (exponentials / totals).astype(jnp.bfloat16)
        attended = jnp.einsum(
            "kgqt,tkd->qkgd", probabilities, value_low, preferred_element_type=jnp.float32
        )
        return (attended.astype(jnp.bfloat16), row_peak[..., 0] + jnp.log(totals[..., 0]))

    attended_blocks, log_totals = lax.map(attend, jnp.arange(block_count))
    attended_low = attended_blocks.reshape(token_count, D)
    branch = jnp.dot(attended_low, output_matrix, preferred_element_type=jnp.float32)
    middle = token_values + branch
    normed_two, root_two = normalize_parts(middle)
    input_two = (normed_two * gain_second).astype(jnp.bfloat16)
    gate_pre = jnp.dot(input_two, gate_matrix, preferred_element_type=jnp.float32)
    up_pre = jnp.dot(input_two, up_matrix, preferred_element_type=jnp.float32)
    sigmoid_gate = jax.nn.sigmoid(gate_pre)
    silu_gate = gate_pre * sigmoid_gate
    product_low = (silu_gate * up_pre).astype(jnp.bfloat16)
    result = middle + jnp.dot(product_low, down_matrix, preferred_element_type=jnp.float32)
    output_tokens = (result * live_rows).astype(jnp.bfloat16)
    regathered = (
        lax.all_gather(w_query, "fsdp", axis=0, tiled=True),
        lax.all_gather(w_key, "fsdp", axis=0, tiled=True),
        lax.all_gather(w_value, "fsdp", axis=0, tiled=True),
        lax.all_gather(w_output, "fsdp", axis=0, tiled=True),
        lax.all_gather(w_gate, "fsdp", axis=0, tiled=True),
        lax.all_gather(w_up, "fsdp", axis=0, tiled=True),
        lax.all_gather(w_down, "fsdp", axis=0, tiled=True),
        lax.all_gather(gains, "fsdp", axis=0, tiled=True),
    )
    back_weights = unpack(regathered)
    (
        back_query,
        back_key,
        back_value,
        back_output,
        back_gate,
        back_up,
        back_down,
        back_first,
        back_second,
    ) = back_weights
    grad_result = cotangent.astype(jnp.float32) * live_rows
    grad_down_in = grad_result.astype(jnp.bfloat16)
    grad_down = jnp.einsum(
        "tf,td->fd", product_low, grad_down_in, preferred_element_type=jnp.float32
    )
    grad_product = jnp.einsum(
        "td,fd->tf", grad_down_in, back_down, preferred_element_type=jnp.float32
    )
    grad_gate_pre = (
        grad_product * up_pre * sigmoid_gate * (1.0 + gate_pre * (1.0 - sigmoid_gate))
    ).astype(jnp.bfloat16)
    grad_up_pre = (grad_product * silu_gate).astype(jnp.bfloat16)
    grad_gate = jnp.einsum(
        "td,tf->df", input_two, grad_gate_pre, preferred_element_type=jnp.float32
    )
    grad_up = jnp.einsum("td,tf->df", input_two, grad_up_pre, preferred_element_type=jnp.float32)
    grad_input_two = jnp.einsum(
        "tf,df->td", grad_gate_pre, back_gate, preferred_element_type=jnp.float32
    )
    grad_input_two = grad_input_two + jnp.einsum(
        "tf,df->td", grad_up_pre, back_up, preferred_element_type=jnp.float32
    )
    grad_gain_two = jnp.sum(grad_input_two * normed_two, axis=0)
    grad_middle = grad_result + norm_backward(grad_input_two, normed_two, root_two, back_second)
    grad_branch = grad_middle.astype(jnp.bfloat16)
    grad_output = jnp.einsum(
        "td,te->de", attended_low, grad_branch, preferred_element_type=jnp.float32
    )
    grad_attended = jnp.einsum(
        "te,de->td", grad_branch, back_output, preferred_element_type=jnp.float32
    ).astype(jnp.bfloat16)
    grad_attended = grad_attended.reshape(token_count, KV_HEADS, group_size, HEAD_DIM)

    def back_step(carried, inputs):
        grad_keys, grad_values = carried
        block_index, log_block = inputs
        query_block, scores = masked_scores()
        probabilities = jnp.exp(scores - log_block[..., None])
        grad_probs = jnp.einsum(
            "qkgd,tkd->kgqt", grad_attended, value_low, preferred_element_type=jnp.float32
        )
        centre = jnp.sum(probabilities * grad_probs, axis=-1, keepdims=True)
        grad_scores = (probabilities * (grad_probs - centre)).astype(jnp.bfloat16)
        grad_query_block = (
            jnp.einsum("kgqt,tkd->qkgd", grad_scores, key_low, preferred_element_type=jnp.float32)
            * score_scale
        )
        grad_keys = (
            grad_keys
            + jnp.einsum(
                "kgqt,qkgd->tkd", grad_scores, query_block, preferred_element_type=jnp.float32
            )
            * score_scale
        )
        grad_values = grad_values + jnp.einsum(
            "kgqt,qkgd->tkd",
            probabilities.astype(jnp.bfloat16),
            grad_attended,
            preferred_element_type=jnp.float32,
        )
        return ((grad_keys, grad_values), grad_query_block)

    zero_state = jnp.zeros((token_count, KV_HEADS, HEAD_DIM), jnp.float32)
    (grad_keys, grad_values), grad_query_blocks = lax.scan(
        back_step, (zero_state, zero_state), (jnp.arange(block_count), log_totals)
    )
    grad_query_low = rotate_back(
        grad_query_blocks.reshape(token_count, HEADS, HEAD_DIM), cosine, sine_table
    )
    grad_query_low = grad_query_low.astype(jnp.bfloat16).reshape(token_count, D)
    grad_key_low = (
        rotate_back(grad_keys, cosine, sine_table).astype(jnp.bfloat16).reshape(token_count, KV)
    )
    grad_value_low = grad_values.astype(jnp.bfloat16).reshape(token_count, KV)
    grad_query = jnp.einsum(
        "td,te->de", input_one, grad_query_low, preferred_element_type=jnp.float32
    )
    grad_key = jnp.einsum("td,te->de", input_one, grad_key_low, preferred_element_type=jnp.float32)
    grad_value = jnp.einsum(
        "td,te->de", input_one, grad_value_low, preferred_element_type=jnp.float32
    )
    grad_input_one = jnp.einsum(
        "te,de->td", grad_query_low, back_query, preferred_element_type=jnp.float32
    )
    grad_input_one = grad_input_one + jnp.einsum(
        "te,de->td", grad_key_low, back_key, preferred_element_type=jnp.float32
    )
    grad_input_one = grad_input_one + jnp.einsum(
        "te,de->td", grad_value_low, back_value, preferred_element_type=jnp.float32
    )
    grad_gain_one = jnp.sum(grad_input_one * normed_one, axis=0)
    grad_tokens = grad_middle + norm_backward(grad_input_one, normed_one, root_one, back_first)
    grad_gains = jnp.concatenate(
        [grad_gain_one, grad_gain_two, jnp.zeros((gain_length - 2 * D,), jnp.float32)]
    )
    shares = (
        lax.psum_scatter(grad_query.reshape(-1), "fsdp", scatter_dimension=0, tiled=True),
        lax.psum_scatter(grad_key.reshape(-1), "fsdp", scatter_dimension=0, tiled=True),
        lax.psum_scatter(grad_value.reshape(-1), "fsdp", scatter_dimension=0, tiled=True),
        lax.psum_scatter(grad_output.reshape(-1), "fsdp", scatter_dimension=0, tiled=True),
        lax.psum_scatter(grad_gate.reshape(-1), "fsdp", scatter_dimension=0, tiled=True),
        lax.psum_scatter(grad_up.reshape(-1), "fsdp", scatter_dimension=0, tiled=True),
        lax.psum_scatter(grad_down.reshape(-1), "fsdp", scatter_dimension=0, tiled=True),
        lax.psum_scatter(grad_gains, "fsdp", scatter_dimension=0, tiled=True),
    )
    return (
        output_tokens,
        grad_tokens.astype(jnp.bfloat16),
        shares[0],
        shares[1],
        shares[2],
        shares[3],
        shares[4],
        shares[5],
        shares[6],
        shares[7],
    )


AXIS_SIZES = (4, 2, 2, 2)
ARRAYS = 4
WIDE = 1536
NARROW = 640
SHAPES = ((16, WIDE), (16, WIDE), (16, WIDE), (64, NARROW))
MESH = pl.DeviceIdType.MESH
PIECES = (
    (0, 0, 16, 0, 768, (1, 0, 2)),
    (0, 0, 16, 768, 768, (2, 0, 1)),
    (1, 0, 16, 0, 768, (1, 0, 2)),
    (1, 0, 16, 768, 768, (2, 0, 1)),
    (2, 0, 16, 0, 768, (0, 1, 2)),
    (2, 0, 16, 768, 768, (0, 2, 1)),
    (3, 0, 32, 0, NARROW, (0, 1, 2)),
    (3, 32, 32, 0, NARROW, (0, 2, 1)),
)


def window(piece):
    return (pl.ds(piece[1], piece[2]), pl.ds(piece[3], piece[4]))


def coordinates():
    me = lax.axis_index("fsdp")
    return [me // 8, (me // 4) % 2, (me // 2) % 2, me % 2]


def device_at(coords):
    return ((coords[0] * 2 + coords[1]) * 2 + coords[2]) * 2 + coords[3]


def peers_along(coords, dim):
    found = []
    for offset in range(1, AXIS_SIZES[dim]):
        other = list(coords)
        other[dim] = lax.rem(coords[dim] + offset, AXIS_SIZES[dim])
        found.append(other)
    return found


def enter(coords):
    barrier = pltpu.get_barrier_semaphore()
    count = 0
    for dim in range(4):
        for other in peers_along(coords, dim):
            pl.semaphore_signal(barrier, inc=1, device_id=(device_at(other),), device_id_type=MESH)
            count += 1
    pl.semaphore_wait(barrier, count)


def gather_kernel(*refs):
    ins, outs = refs[:ARRAYS], refs[ARRAYS : 2 * ARRAYS]
    send_sem, recv_sem = refs[2 * ARRAYS :]
    coords = coordinates()
    enter(coords)

    for which in range(ARRAYS):
        outs[which][coords[0], coords[1], coords[2], coords[3]] = ins[which][...]

    def run(which, piece):
        out = outs[piece[0]]
        counter = [0]
        index = list(coords)
        sibling = peers_along(coords, 3)[0]
        core_copies = []

        def push(block, target):
            slot = counter[0]
            counter[0] += 1
            view = out.at[tuple(block) + window(piece)]
            copy = pltpu.make_async_remote_copy(
                src_ref=view,
                dst_ref=view,
                send_sem=send_sem.at[which, slot],
                recv_sem=recv_sem.at[which, slot],
                device_id=(device_at(target),),
                device_id_type=MESH,
            )
            copy.start()
            return copy

        pending_core = [list(index)]
        for dim in piece[5]:
            copies = [push(index, other) for other in peers_along(coords, dim)]
            for block in pending_core:
                core_copies.append(push(block, sibling))
            pending_core = []
            yield
            for offset, copy in enumerate(copies):
                copy.wait()
                block = list(index)
                size = AXIS_SIZES[dim]
                block[dim] = lax.rem(coords[dim] + size - offset - 1, size)
                pending_core.append(block)
            index[dim] = slice(None)
        for block in pending_core:
            core_copies.append(push(block, sibling))
        yield
        for copy in core_copies:
            copy.wait()

    drive([run(which, piece) for which, piece in enumerate(PIECES)])


def drive(tasks):
    while tasks:
        kept = []
        for task in tasks:
            try:
                next(task)
                kept.append(task)
            except StopIteration:
                pass
        tasks = kept


def scatter_kernel(*refs):
    ins, outs = refs[:ARRAYS], refs[ARRAYS : 2 * ARRAYS]
    landing = refs[2 * ARRAYS : -2]
    send_sem, recv_sem = refs[-2:]
    coords = coordinates()
    enter(coords)

    def run(which, piece):
        order = (3,) + tuple(reversed(piece[5]))
        remaining = [0, 1, 2, 3]
        current = ins[piece[0]]
        counter = [0]

        def push(stage, dim, part, offset, target):
            slot = counter[0]
            counter[0] += 1
            index = tuple(
                part if axis == dim else slice(None) for axis in remaining
            )
            if stage == 0:
                index = index + window(piece)
            land = landing[which * 4 + stage]
            copy = pltpu.make_async_remote_copy(
                src_ref=current.at[index],
                dst_ref=land.at[offset],
                send_sem=send_sem.at[which, slot],
                recv_sem=recv_sem.at[which, slot],
                device_id=(device_at(target),),
                device_id_type=MESH,
            )
            copy.start()
            return copy

        copies = [
            push(0, 3, other[3], offset, other)
            for offset, other in enumerate(peers_along(coords, 3))
        ]
        for stage, dim in enumerate(order):
            yield
            for copy in copies:
                copy.wait()
            land = landing[which * 4 + stage]
            rest = [axis for axis in remaining if axis != dim]
            last = stage == 3

            def add_group(fixed, current=current, land=land, rest=rest, dim=dim, last=last, held=tuple(remaining), first=stage == 0):
                loose = [axis for axis in rest if axis not in fixed]
                total = 1
                for axis in loose:
                    total *= AXIS_SIZES[axis]

                def body(step, carry):
                    at = dict(fixed)
                    left = step
                    for axis in reversed(loose):
                        at[axis] = left % AXIS_SIZES[axis]
                        left = left // AXIS_SIZES[axis]
                    mine = tuple(coords[dim] if axis == dim else at[axis] for axis in held)
                    target = tuple(at[axis] for axis in rest)
                    if first:
                        mine = mine + window(piece)
                    value = current[mine].astype(jnp.float32)
                    for offset in range(AXIS_SIZES[dim] - 1):
                        value = value + land[(offset,) + target].astype(jnp.float32)
                    if last:
                        outs[piece[0]][window(piece)] = value
                    else:
                        land[(0,) + target] = value.astype(jnp.bfloat16)
                    return carry

                if total == 1:
                    body(0, 0)
                else:
                    lax.fori_loop(0, total, body, 0)

            if last:
                add_group({})
                break
            following = order[stage + 1]
            remaining = rest
            current = land.at[0]
            copies = []
            for offset, other in enumerate(peers_along(coords, following)):
                add_group({following: other[following]})
                copies.append(push(stage + 1, following, other[following], offset, other))
            add_group({following: coords[following]})

    drive([run(which, piece) for which, piece in enumerate(PIECES)])


def gather_packed(parts):
    return pl.pallas_call(
        gather_kernel,
        out_shape=tuple(jax.ShapeDtypeStruct(AXIS_SIZES + shape, jnp.bfloat16) for shape in SHAPES),
        in_specs=[pl.BlockSpec(memory_space=pltpu.VMEM)] * ARRAYS,
        out_specs=tuple([pl.BlockSpec(memory_space=pltpu.VMEM)] * ARRAYS),
        scratch_shapes=[
            pltpu.SemaphoreType.DMA((len(PIECES), 12)),
            pltpu.SemaphoreType.DMA((len(PIECES), 12)),
        ],
        compiler_params=pltpu.CompilerParams(
            collective_id=0, has_side_effects=True, vmem_limit_bytes=12 * 1024 * 1024
        ),
        name="gather_weights",
    )(*parts)


def scatter_packed(parts):
    landing = []
    for piece in PIECES:
        remaining = [0, 1, 2, 3]
        for dim in (3,) + tuple(reversed(piece[5])):
            remaining = [axis for axis in remaining if axis != dim]
            extent = tuple(AXIS_SIZES[axis] for axis in remaining)
            landing.append(
                pltpu.VMEM((AXIS_SIZES[dim] - 1,) + extent + (piece[2], piece[4]), jnp.bfloat16)
            )
    return pl.pallas_call(
        scatter_kernel,
        out_shape=tuple(jax.ShapeDtypeStruct(shape, jnp.float32) for shape in SHAPES),
        in_specs=[pl.BlockSpec(memory_space=pltpu.VMEM)] * ARRAYS,
        out_specs=tuple([pl.BlockSpec(memory_space=pltpu.VMEM)] * ARRAYS),
        scratch_shapes=landing
        + [
            pltpu.SemaphoreType.DMA((len(PIECES), 8)),
            pltpu.SemaphoreType.DMA((len(PIECES), 8)),
        ],
        compiler_params=pltpu.CompilerParams(
            collective_id=1, has_side_effects=True, vmem_limit_bytes=20 * 1024 * 1024
        ),
        name="scatter_gradients",
    )(*parts)


DEVICES = 32
ROWS = D // DEVICES
DOWN_ROWS = FF // DEVICES
SPILL = ROWS - 16


STREAM = 640
CHUNK = 512
PER_GAIN = 36


def order_matrices():
    main = (np.arange(DEVICES)[:, None] * ROWS + np.arange(16)[None, :]).reshape(-1)
    spill = (np.arange(DEVICES)[:, None] * ROWS + 16 + np.arange(SPILL)[None, :]).reshape(-1)
    stream = np.zeros((D, STREAM), np.float32)
    stream[main, np.arange(512)] = 1.0
    stream[spill, 576 + np.arange(64)] = 1.0
    columns = np.concatenate([stream[:, 576:], stream[:, :512]], axis=1)
    select = np.zeros((512, 512), np.float32)
    for part in range(8):
        for owner in range(DEVICES):
            for row in range(SPILL):
                select[part * 64 + owner * 2 + row, owner * 16 + row * 8 + part] = 1.0
    true_index = np.full((STREAM,), -1)
    true_index[:512] = main
    true_index[576:] = spill
    pick = np.zeros((2, 64, STREAM), np.float32)
    holder = np.zeros((2, 64, STREAM), np.float32)
    for half in range(2):
        for lane in range(STREAM):
            if true_index[lane] >= 0:
                flat = half * D + true_index[lane]
                pick[half, flat % PER_GAIN, lane] = 1.0
                holder[half, 2 * (flat // PER_GAIN), lane] = 1.0
    return tuple(value.astype(ml_dtypes.bfloat16) for value in (stream, columns, select, pick, holder))


def dot(left, right, contract=(1, 0), precision=None):
    return lax.dot_general(
        left,
        right,
        (((contract[0],), (contract[1],)), ((), ())),
        preferred_element_type=jnp.float32,
        precision=precision,
    )


def low_dot(left, right, contract=(1, 0)):
    return dot(left, right, contract).astype(jnp.bfloat16)


def swap_halves(values):
    width = values.shape[1]
    lane = lax.broadcasted_iota(jnp.int32, values.shape, 1)
    return jnp.where(
        lane % HEAD_DIM < HEAD_DIM // 2,
        pltpu.roll(values, width - HEAD_DIM // 2, 1),
        pltpu.roll(values, HEAD_DIM // 2, 1),
    )


def stream_norm(values):
    root = lax.rsqrt(jnp.sum(values * values, axis=1, keepdims=True) * (1.0 / D) + NORM_EPSILON)
    return values * root, root


def stream_norm_back(grad_in, normed, root, gain_row):
    scaled = grad_in * gain_row
    mean = jnp.sum(scaled * normed, axis=1, keepdims=True) * (1.0 / D)
    return root * (scaled - normed * mean)


def layer_kernel(
    tokens, cotangent, seg_row, seg_col, cosine, sine, stream, select, pick, holder,
    mixed, gate, up, extra,
    out_tokens, out_grad_tokens, g_mixed, g_gate, g_up, g_extra,
    w_spill, w_down, g_spill, probs, heads, attended, g_heads, result, g_input,
):
    low = jnp.bfloat16
    count = tokens.shape[0]
    scale = HEAD_DIM ** (-0.5)
    spill_in = extra[:, :16, :].reshape(512, STREAM)
    spill_rows = low_dot(select[...], spill_in)
    w_spill[0:64, :] = jnp.zeros((64, 8 * STREAM), low)
    for part in range(8):
        w_spill[64:128, part * STREAM : (part + 1) * STREAM] = spill_rows[part * 64 : part * 64 + 64]
    w_down[...] = extra[:, 16:, :].reshape(FF, STREAM)
    gain_block = spill_rows[448:512, 128:192]
    gains = [
        jnp.sum(dot(gain_block, pick[half]) * holder[half].astype(jnp.float32), axis=0, keepdims=True)
        for half in range(2)
    ]

    values = dot(tokens[...], stream[...])
    live = (seg_col[...] >= 0).astype(jnp.float32)
    grad_result = dot(cotangent[...], stream[...]) * live
    grad_down_in = grad_result.astype(low)
    normed_one, root_one = stream_norm(values)
    input_one = (normed_one * gains[0]).astype(low)
    one_main, one_spill = input_one[:, :512], input_one[:, 512:]
    qkv = dot(one_main, mixed[:, :1024]) + dot(one_spill, w_spill[:, :1024])
    wide_cos = jnp.concatenate([cosine[...]] * 6, axis=1)
    wide_sin = jnp.concatenate([sine[...]] * 6, axis=1)
    turning = qkv[:, :768]
    heads[:, :768] = (turning * wide_cos + swap_halves(turning) * wide_sin).astype(low)
    heads[:, 768:] = qkv[:, 768:].astype(low)
    column = lax.broadcasted_iota(jnp.int32, (count, count), 1)
    row = lax.broadcasted_iota(jnp.int32, (count, count), 0)
    allowed = (seg_col[...] == seg_row[...]) & (column <= row)

    def head(array, start):
        return array[:, start : start + HEAD_DIM]

    for h in range(HEADS):
        c = h // 3
        scores = dot(head(heads, 64 * h), head(heads, 576 + 64 * c), (1, 1)) * scale
        scores = jnp.where(allowed, scores, NEG_LARGE)
        peak = jnp.max(scores, axis=1, keepdims=True)
        powers = jnp.exp(scores - peak)
        p = powers / jnp.sum(powers, axis=1, keepdims=True)
        probs[h] = p
        attended[:, 64 * h : 64 * h + 64] = low_dot(p.astype(low), head(heads, 768 + 64 * c))
    att = low_dot(attended[...], stream[...])
    att_main, att_spill = att[:, :512], att[:, 512:]
    branch_main = dot(att_main, mixed[:, 1024:]) + dot(att_spill, w_spill[:, 1024:1536])
    branch_spill = dot(att_main, mixed[:, 896:1024]) + dot(att_spill, w_spill[:, 896:1024])
    lane = lax.broadcasted_iota(jnp.int32, branch_spill.shape, 1)
    branch_spill = jnp.where(lane >= 64, branch_spill, 0.0)
    middle = values + jnp.concatenate([branch_main, branch_spill], axis=1)
    normed_two, root_two = stream_norm(middle)
    input_two = (normed_two * gains[1]).astype(low)
    two_main, two_spill = input_two[:, :512], input_two[:, 512:]
    result[...] = middle
    g_input[...] = jnp.zeros_like(g_input)

    for start in range(0, FF, CHUNK):
        here = slice(start, start + CHUNK)
        gate_at = slice(FF + start, FF + start + CHUNK)
        up_at = slice(2 * FF + start, 2 * FF + start + CHUNK)
        gate_pre = dot(two_main, gate[:, here]) + dot(two_spill, w_spill[:, gate_at])
        up_pre = dot(two_main, up[:, here]) + dot(two_spill, w_spill[:, up_at])
        sig = 1.0 / (1.0 + jnp.exp(-gate_pre))
        silu = gate_pre * sig
        product = (silu * up_pre).astype(low)
        down = w_down[here, :]
        result[...] += dot(product, down)
        w_down_grad = low_dot(product, grad_down_in, (0, 0))
        g_product = dot(grad_down_in, down, (1, 1))
        gg = (g_product * up_pre * sig * (1.0 + gate_pre * (1.0 - sig))).astype(low)
        gu = (g_product * silu).astype(low)
        g_input[:, :512] += dot(gg, gate[:, here], (1, 1)) + dot(gu, up[:, here], (1, 1))
        g_input[:, 512:] += dot(gg, w_spill[:, gate_at], (1, 1)) + dot(gu, w_spill[:, up_at], (1, 1))
        g_gate[:, here] = low_dot(two_main, gg, (0, 0))
        g_up[:, here] = low_dot(two_main, gu, (0, 0))
        g_spill[:, gate_at] = low_dot(two_spill, gg, (0, 0))[64:]
        g_spill[:, up_at] = low_dot(two_spill, gu, (0, 0))[64:]
        w_down[here, :] = w_down_grad
    g_extra[:, 16:, :] = w_down[...].reshape(DEVICES, DOWN_ROWS, STREAM)
    out_tokens[...] = low_dot((result[...] * live).astype(low), stream[...], (1, 1))

    grad_input_two = g_input[...]
    gain_grads = [None, jnp.sum(grad_input_two * normed_two, axis=0, keepdims=True)]
    grad_middle = grad_result + stream_norm_back(grad_input_two, normed_two, root_two, gains[1])
    grad_branch = grad_middle.astype(low)
    branch_main, branch_spill = grad_branch[:, :512], grad_branch[:, 512:]
    g_mixed[:, 1024:] = low_dot(att_main, branch_main, (0, 0))
    g_spill[:, 1024:1536] = low_dot(att_spill, branch_main, (0, 0))[64:]
    g_att = jnp.concatenate(
        [
            dot(branch_main, mixed[:, 1024:], (1, 1)) + dot(branch_spill, mixed[:, 896:1024], (1, 1)),
            dot(branch_main, w_spill[:, 1024:1536], (1, 1))
            + dot(branch_spill, w_spill[:, 896:1024], (1, 1)),
        ],
        axis=1,
    )
    attended[...] = low_dot(g_att.astype(low), stream[...], (1, 1))
    g_heads[:, 896:] = jnp.zeros((count, 128), jnp.float32)
    for c in range(KV_HEADS):
        keys, vals = head(heads, 576 + 64 * c), head(heads, 768 + 64 * c)
        g_keys, g_vals = 0.0, 0.0
        for h in range(3 * c, 3 * c + 3):
            p, g_a, q = probs[h], head(attended, 64 * h), head(heads, 64 * h)
            gp = dot(g_a, vals, (1, 1))
            centre = jnp.sum(p * gp, axis=1, keepdims=True)
            gs = (p * (gp - centre)).astype(low)
            g_heads[:, 64 * h : 64 * h + 64] = dot(gs, keys) * scale
            g_keys = g_keys + dot(gs, q, (0, 0))
            g_vals = g_vals + dot(p.astype(low), g_a, (0, 0))
        g_heads[:, 576 + 64 * c : 640 + 64 * c] = g_keys * scale
        g_heads[:, 768 + 64 * c : 832 + 64 * c] = g_vals
    turning = g_heads[:, :768]
    grad_qkv = jnp.concatenate(
        [turning * wide_cos - swap_halves(turning) * wide_sin, g_heads[:, 768:]], axis=1
    ).astype(low)
    g_mixed[:, :896] = low_dot(one_main, grad_qkv[:, :896], (0, 0))
    g_spill[:, :896] = low_dot(one_spill, grad_qkv[:, :896], (0, 0))[64:]
    tail = grad_qkv[:, 896:]
    g_mixed[:, 896:1024] = (dot(one_main, tail, (0, 0)) + dot(att_main, branch_spill, (0, 0))).astype(low)
    g_spill[:, 896:1024] = (dot(one_spill, tail, (0, 0)) + dot(att_spill, branch_spill, (0, 0))).astype(low)[64:]
    grad_input_one = jnp.concatenate(
        [dot(grad_qkv, mixed[:, :1024], (1, 1)), dot(grad_qkv, w_spill[:, :1024], (1, 1))], axis=1
    )
    gain_grads[0] = jnp.sum(grad_input_one * normed_one, axis=0, keepdims=True)
    grad_tokens = grad_middle + stream_norm_back(grad_input_one, normed_one, root_one, gains[0])
    out_grad_tokens[...] = low_dot(grad_tokens.astype(low), stream[...], (1, 1))
    block = 0.0
    for half in range(2):
        spread = holder[half].astype(jnp.float32) * gain_grads[half]
        block = block + dot(spread.astype(low), pick[half], (1, 1))
    g_spill[:, 3 * FF :] = jnp.concatenate(
        [block, jnp.zeros((64, 8 * STREAM - 3 * FF - 64), jnp.float32)], axis=1
    ).astype(low)
    stacked = jnp.concatenate(
        [g_spill[:, part * STREAM : (part + 1) * STREAM] for part in range(8)], axis=0
    )
    g_extra[:, :16, :] = low_dot(select[...], stacked, (0, 0)).reshape(DEVICES, 16, STREAM)


def local_layer(*operands):
    count = operands[0].shape[0]
    low = jnp.bfloat16
    vmem = pl.BlockSpec(memory_space=pltpu.VMEM)
    return pl.pallas_call(
        layer_kernel,
        out_shape=(
            jax.ShapeDtypeStruct((count, D), low),
            jax.ShapeDtypeStruct((count, D), low),
            jax.ShapeDtypeStruct((512, WIDE), low),
            jax.ShapeDtypeStruct((512, WIDE), low),
            jax.ShapeDtypeStruct((512, WIDE), low),
            jax.ShapeDtypeStruct((DEVICES, 64, STREAM), low),
        ),
        in_specs=[vmem] * len(operands),
        out_specs=(vmem,) * 6,
        scratch_shapes=[
            pltpu.VMEM((128, 8 * STREAM), low),
            pltpu.VMEM((FF, STREAM), low),
            pltpu.VMEM((64, 8 * STREAM), low),
            pltpu.VMEM((HEADS, count, count), jnp.float32),
            pltpu.VMEM((count, 1024), low),
            pltpu.VMEM((count, D), low),
            pltpu.VMEM((count, 1024), jnp.float32),
            pltpu.VMEM((count, STREAM), jnp.float32),
            pltpu.VMEM((count, STREAM), jnp.float32),
        ],
        compiler_params=pltpu.CompilerParams(vmem_limit_bytes=34 * 1024 * 1024),
        name="local_layer",
    )(*operands)


def packed_device(
    tokens, segments, w_query, w_key, w_value, w_output, w_gate, w_up, w_down, gains, cotangent
):
    token_count = tokens.shape[0]
    stream, columns, select, pick, holder = (jnp.asarray(value) for value in order_matrices())
    share = gains.shape[0]
    rows = jnp.concatenate(
        [
            w_query.reshape(ROWS, D),
            w_key.reshape(ROWS, KV),
            w_value.reshape(ROWS, KV),
            low_dot(w_output.reshape(ROWS, D), columns),
            w_gate.reshape(ROWS, FF),
            w_up.reshape(ROWS, FF),
        ],
        axis=1,
    )
    down_rows = low_dot(w_down.reshape(DOWN_ROWS, D), stream)
    spare = jnp.pad(gains.reshape(1, share), ((0, 1), (0, 8 * STREAM - 3 * FF - share)))
    spill = jnp.concatenate([rows[16:], spare], axis=1).reshape(16, STREAM)
    weights = gather_packed(
        (
            rows[:16, :WIDE],
            rows[:16, WIDE : 2 * WIDE],
            rows[:16, 2 * WIDE :],
            jnp.concatenate([spill, down_rows], axis=0),
        )
    )
    column = jnp.arange(token_count)[None, :]
    row_index = jnp.arange(token_count)[:, None]
    same_segment = segments[:, None] == segments[None, :]
    positions = jnp.sum((same_segment & (column < row_index)).astype(jnp.int32), axis=1)
    frequency = ROPE_BASE ** (-(2.0 * jnp.arange(HEAD_DIM // 2).astype(jnp.float32)) / HEAD_DIM)
    angles = positions.astype(jnp.float32)[:, None] * frequency[None, :]
    cosine, sine = jnp.cos(angles), jnp.sin(angles)
    output_tokens, grad_tokens, g_mixed, g_gate, g_up, g_extra = local_layer(
        tokens,
        cotangent,
        segments[None, :],
        segments[:, None],
        jnp.concatenate([cosine] * 4, axis=1),
        jnp.concatenate([-sine, sine, -sine, sine], axis=1),
        stream,
        select,
        pick,
        holder,
        weights[0].reshape(512, WIDE),
        weights[1].reshape(512, WIDE),
        weights[2].reshape(512, WIDE),
        weights[3].reshape(DEVICES, 64, STREAM),
    )
    mixed, gate_part, up_part, extra = scatter_packed(
        (
            g_mixed.reshape(AXIS_SIZES + SHAPES[0]),
            g_gate.reshape(AXIS_SIZES + SHAPES[1]),
            g_up.reshape(AXIS_SIZES + SHAPES[2]),
            g_extra.reshape(AXIS_SIZES + SHAPES[3]),
        )
    )
    spill = extra[:16].reshape(SPILL, 8 * STREAM)
    mixed = jnp.concatenate([mixed, spill[:, :WIDE]], axis=0)
    exact = lax.Precision.HIGHEST
    return (
        output_tokens,
        grad_tokens,
        mixed[:, :D].reshape(-1),
        mixed[:, D : D + KV].reshape(-1),
        mixed[:, D + KV : D + 2 * KV].reshape(-1),
        dot(mixed[:, D + 2 * KV :], columns.astype(jnp.float32), (1, 1), exact).reshape(-1),
        jnp.concatenate([gate_part, spill[:, WIDE : 2 * WIDE]], axis=0).reshape(-1),
        jnp.concatenate([up_part, spill[:, 2 * WIDE : 3 * WIDE]], axis=0).reshape(-1),
        dot(extra[16:], stream.astype(jnp.float32), (1, 1), exact).reshape(-1),
        extra[7, 128 : 128 + share],
    )


def solution(mesh):
    placed = (
        P("fsdp", None),
        P("fsdp"),
        P("fsdp"),
        P("fsdp"),
        P("fsdp"),
        P("fsdp"),
        P("fsdp"),
        P("fsdp"),
        P("fsdp"),
        P("fsdp"),
        P("fsdp", None),
    )
    return jax.shard_map(
        packed_device if mesh.shape["fsdp"] == DEVICES else per_device,
        mesh=mesh,
        in_specs=placed,
        out_specs=(
            P("fsdp", None),
            P("fsdp", None),
            P("fsdp"),
            P("fsdp"),
            P("fsdp"),
            P("fsdp"),
            P("fsdp"),
            P("fsdp"),
            P("fsdp"),
            P("fsdp"),
        ),
        check_vma=False,
    )
```
